256 devices in a mesh: ctx: 32 (over z, x_hi, core), head: 8 (over y, x_lo).
Axes of the slice: x: 4 (x_hi: 2, x_lo: 2; x = x_hi * 2 + x_lo), y: 4, z: 8, core: 2. Of those that a mesh axis runs over, the one named last changes fastest.
Arguments:
- queries: bfloat16 [4096, 64, 192], P('ctx', 'head'), may hold values from -8 to 8
- latent: bfloat16 [4096, 512], P('ctx'), may hold values from -6 to 6
- key_rope: bfloat16 [4096, 64], P('ctx'), may hold values from -8 to 8
- up_keys: bfloat16 [512, 64, 128], P(None, 'head'), may hold values from -0.25 to 0.25
- up_values: bfloat16 [512, 64, 128], P(None, 'head'), may hold values from -0.25 to 0.25
- out_weight: bfloat16 [8192, 7168], P('head', 'ctx'), may hold values from -1 to 1
- block_order: int32 [64], replicated, may hold values from 0 to 63, each once
Outputs:
- mixed: bfloat16 [4096, 7168], P('ctx', 'head')
The draws below stay inside these ranges and needn't reach their ends.
Inputs may be any that keep to these rules, and one draw needn't show every extreme that they name: A permutation; row r of the prompt lies in position block block_order[r // 64].
All inputs are finite; a program needn't handle non-finite values.
Results may differ from the reference program's by a relative error of at most 0.019.
Values may be sent and summed in bfloat16 or wider, within the bound.
A program may use at most 128 MiB of HBM per device.

```python
import jax
import jax.numpy as jnp
from jax import lax

D = 7168
H = 64
LATENT = 512
NOPE = 128
ROPE = 64
VDIM = 128
HALF = 64
SEQ = 4096
BLOCKS = 64


def draw_queries(key, part):
    key = jax.random.fold_in(key, 11)
    first = jax.random.fold_in(key, 0)
    result = jnp.clip(jax.random.normal(first, (SEQ, H, NOPE + ROPE), jnp.float32), -8.0, 8.0)
    return result.astype(jnp.bfloat16)


def draw_key_rope(key, part):
    key = jax.random.fold_in(key, 23)
    result = jnp.clip(jax.random.normal(key, (SEQ, ROPE), jnp.float32), -8.0, 8.0)
    return result.astype(jnp.bfloat16)


def spiked(entries, own_key, source, target, blocks, factor):
    def block_of(dim):
        return (jnp.arange(entries.shape[dim]) // (entries.shape[dim] // blocks)).reshape((-1,) + (1,) * (entries.ndim - 1 - dim))

    one_side = jax.random.permutation(own_key, blocks)[block_of(target)]
    far = (block_of(target) + blocks // 2) % blocks
    return jnp.where((block_of(source) == one_side) | (block_of(source) == far), factor * entries, entries)


def levels(key, shape, pieces, low, high):
    level, own = 1.0, jax.random.fold_in(key, 6)
    for dim, blocks in pieces:
        steps = jnp.exp(jax.random.uniform(jax.random.fold_in(own, dim), (blocks,), jnp.float32, low / len(pieces), high / len(pieces)))
        level = level * jnp.repeat(steps, shape[dim] // blocks).reshape([-1 if axis == dim else 1 for axis in range(len(shape))])
    return level


def bell_draw(key, dims, spread, reach, cuts=(), kind=jnp.bfloat16):
    level = levels(key, dims, cuts, -0.22, 0.18) if cuts else 1.0
    values = jax.random.normal(key, dims, jnp.float32) * spread * level
    return jnp.minimum(jnp.maximum(values, -reach), reach).astype(kind)


def noise_with(stream_key, dims, scale, bound, shards, heavy, kind=jnp.bfloat16):
    values = scale * jax.random.normal(stream_key, dims, jnp.float32)
    if shards:
        values = values * levels(stream_key, dims, shards, -0.22, 0.18)
    return jnp.clip(spiked(values, jax.random.fold_in(stream_key, 3), *heavy), -bound, bound).astype(kind)


def setup_inputs(seed: int = 0) -> dict:
    key_of = jax.random.split(jax.random.key(seed), 8)
    queries = draw_queries(jax.random.fold_in(key_of[7], 71), 0)
    latent = bell_draw(key_of[1], (SEQ, LATENT), 1.0, 6.0, ((0, 32),))
    key_rope = draw_key_rope(jax.random.fold_in(key_of[7], 71), 0)
    up_keys = bell_draw(key_of[3], (LATENT, H, NOPE), LATENT ** -0.5, 0.25, ((1, 8),))
    up_values = bell_draw(key_of[4], (LATENT, H, VDIM), LATENT ** -0.5, 0.25, ((1, 8),))
    out_weight = noise_with(key_of[5], (H * VDIM, D), (H * 2) ** -0.5, 1.0, ((0, 8), (1, 32)), (0, 1, 32, 2.75))
    block_order = jax.random.permutation(key_of[6], BLOCKS).astype(jnp.int32)
    return {"queries": queries, "latent": latent, "key_rope": key_rope, "up_keys": up_keys, "up_values": up_values, "out_weight": out_weight, "block_order": block_order}


def positions_of(block_order, count, half_rows):
    indices = jnp.arange(count, dtype=jnp.int32)
    return block_order[indices // half_rows] * half_rows + indices % half_rows


def reference(queries, latent, key_rope, up_keys, up_values, out_weight, block_order):
    position = positions_of(block_order, SEQ, HALF)
    visible = position[None, :] <= position[:, None]
    scale = (NOPE + ROPE) ** -0.5

    def one_head(head_number):
        keys = jnp.dot(latent, up_keys[:, head_number, :], preferred_element_type=jnp.float32).astype(jnp.bfloat16)
        values = jnp.dot(latent, up_values[:, head_number, :], preferred_element_type=jnp.float32).astype(jnp.bfloat16)
        query = queries[:, head_number, :]
        scores = jnp.dot(query[:, :NOPE], keys.T, preferred_element_type=jnp.float32)
        scores = scores + jnp.dot(query[:, NOPE:], key_rope.T, preferred_element_type=jnp.float32)
        scores = jnp.where(visible, scores * scale, -jnp.inf)
        largest = jnp.max(scores, axis=1, keepdims=True)
        powers = jnp.exp(scores - largest)
        total = jnp.dot(powers.astype(jnp.bfloat16), values, preferred_element_type=jnp.float32)
        return (total / jnp.sum(powers, axis=1, keepdims=True)).astype(jnp.bfloat16)

    attended = lax.map(one_head, jnp.arange(H, dtype=jnp.int32))
    attended = jnp.transpose(attended, (1, 0, 2)).reshape(SEQ, H * VDIM)
    return jnp.dot(attended, out_weight, preferred_element_type=jnp.float32).astype(jnp.bfloat16)
```

```python
import functools

import jax
import jax.numpy as jnp
from jax import lax
from jax.experimental import pallas as pl
from jax.experimental.pallas import tpu as pltpu
from jax.sharding import PartitionSpec as P

MESH = pl.DeviceIdType.MESH
F32 = jnp.float32
BF16 = jnp.bfloat16
NT = (((1,), (1,)), ((), ()))
LOW = -1e30


def wait(ref, sem):
    pltpu.make_async_copy(ref, ref, sem).wait()


def kernel(
    q_ref, lat_ref, rope_ref, uk_ref, uv_ref, w_ref, order_ref, out_ref,
    lat, keys, qp, bias, acc, top, total, w_in, w1, w2, att, part, got, summed, turned, final,
    x_sem, w_sem, lz_send, lz_recv, ls_send, ls_recv, az_send, az_recv, as_send, as_recv,
    c_send, c_recv, t_send, t_recv, f_send, f_recv,
):
    ctx, head = lax.axis_index("ctx"), lax.axis_index("head")
    z, xh, core = ctx // 4, (ctx // 2) % 2, ctx % 2
    y, xl = head // 2, head % 2
    factor = (192.0 ** -0.5) * 1.4426950408889634

    def at(z_, xh_, core_, y_, xl_):
        return (z_ * 4 + xh_ * 2 + core_, y_ * 2 + xl_)

    sibling = at(z, xh, 1 - core, y, xl)
    x_next = at(z, 1 - xh, core, y, 1 - xl)
    x_far = at(z, 1 - xh, core, y, xl)

    def send(src, dst, send_sem, recv_sem, device):
        pltpu.make_async_remote_copy(
            src_ref=src, dst_ref=dst, send_sem=send_sem, recv_sem=recv_sem,
            device_id=device, device_id_type=MESH,
        ).start()

    def other_head(step, core_):
        return at(z, xh, core_, (y + step // 2) % 4, (xl + step) % 2)

    barrier = pltpu.get_barrier_semaphore()
    partners = [sibling, x_next, x_far]
    partners += [at((z + step) % 8, xh, core, y, xl) for step in range(1, 8)]
    partners += [other_head(step, c) for step in range(1, 8) for c in (core, 1 - core)]
    for device in partners:
        pl.semaphore_signal(barrier, inc=1, device_id=device, device_id_type=MESH)

    lat[z, core, xh, 0:128, :] = lat_ref[...]
    rope = rope_ref[...].astype(F32)
    rope = rope[0:64, :] + pltpu.roll(rope[64:128, :], 64, 1)
    for g in range(4):
        lat[z, core, xh, 128:144, g * 128 : (g + 1) * 128] = rope[g * 16 : (g + 1) * 16, :].astype(BF16)

    pl.semaphore_wait(barrier, len(partners))
    mine = lat.at[z, core, xh]
    send(mine, mine, x_sem.at[0], x_sem.at[1], x_next)

    def project(h, carry):
        rows = pl.ds(pl.multiple_of(h * 128, 128), 128)
        qp[rows, 0:512] = lax.dot_general(
            q_ref[h, :, 0:128], uk_ref[h], NT, preferred_element_type=F32
        ).astype(BF16)
        qp[rows, 512:640] = q_ref[h, :, 128:256]
        return carry

    lax.fori_loop(0, 8, project, 0)
    top[...] = jnp.full_like(top, LOW)
    total[...] = jnp.zeros_like(total)
    acc[...] = jnp.zeros_like(acc)
    wait(mine, x_sem.at[1])

    def ring(buf, s, side, z_send, z_recv, s_send, s_recv):
        zz = (z + 8 - s) % 8 if side == 0 else (z + s) % 8
        block = buf.at[zz, core]
        active = (s >= 0) if side == 0 else ((s >= 1) & (s <= 3))

        @pl.when(active & (s > 0))
        def _():
            wait(block, z_recv.at[zz])

        @pl.when((s < 3) | ((s == 3) & (core == side)))
        def _():
            to = (z + 1) % 8 if side == 0 else (z + 7) % 8
            send(block, block, z_send.at[0], z_recv.at[zz], at(to, xh, core, y, xl))

        @pl.when(active)
        def _():
            send(block, block, s_send.at[0], s_recv.at[zz], sibling)

        return zz, active

    lane = lax.broadcasted_iota(jnp.int32, (128, 512), 1)
    row = lax.broadcasted_iota(jnp.int32, (128, 512), 0)

    def attend(zz):
        wait(lat.at[zz, 1 - core], ls_recv.at[zz])
        place = jnp.zeros((128, 512), jnp.int32)
        for c in range(2):
            for x in range(2):
                n = c * 2 + x
                for half in range(2):
                    block = order_ref[zz * 8 + x * 4 + c * 2 + half] * 64
                    place = jnp.where(lane // 64 == n * 2 + half, block + lane % 64, place)
                keys[n * 128 : (n + 1) * 128, 0:512] = lat[zz, c, x, 0:128, :]
                for g in range(4):
                    pair = lat[zz, c, x, 128:144, g * 128 : (g + 1) * 128]
                    keys[n * 128 + g * 16 : n * 128 + g * 16 + 16, 512:640] = pair
                    turn = pltpu.roll(pair.astype(F32), 64, 1).astype(BF16)
                    keys[n * 128 + 64 + g * 16 : n * 128 + 64 + g * 16 + 16, 512:640] = turn
        own = jnp.where(
            row < 64, order_ref[ctx * 2] * 64 + row, order_ref[ctx * 2 + 1] * 64 + row - 64
        )
        bias[...] = jnp.where(place <= own, 0.0, LOW)
        for r in range(4):
            rows = slice(r * 256, (r + 1) * 256)
            s = lax.dot_general(qp[rows, :], keys[...], NT, preferred_element_type=F32)
            s = s + jnp.concatenate([bias[...], bias[...]], axis=0)
            old = top[rows, :]
            new = jnp.maximum(old, jnp.max(s, axis=1, keepdims=True))
            top[rows, :] = new
            p = jnp.exp2((s - new[:, 0:1]) * factor)
            fade = jnp.exp2((old - new) * factor)
            total[rows, :] = total[rows, :] * fade + (
                (p[:, 0:128] + p[:, 128:256]) + (p[:, 256:384] + p[:, 384:512])
            )
            added = jnp.dot(p.astype(BF16), keys[:, 0:512], preferred_element_type=F32)
            acc[rows, :] = acc[rows, :] * fade[:, 0:1] + added

    def gather_step(s, carry):
        z0, on0 = ring(lat, s, 0, lz_send, lz_recv, ls_send, ls_recv)
        z1, on1 = ring(lat, s, 1, lz_send, lz_recv, ls_send, ls_recv)

        @pl.when(s == 1)
        def _():
            send(w_ref, w_in, w_sem.at[0], w_sem.at[1], x_far)

        def one(i, c):
            attend(jnp.where(i == 0, z0, z1))
            return c

        lax.fori_loop(0, jnp.where((s >= 1) & (s <= 3), 2, 1), one, 0)
        return carry

    lax.fori_loop(0, 5, gather_step, 0)

    wait(w_in, w_sem.at[1])

    def widen(i, carry):
        rows = pl.ds(pl.multiple_of(i * 128, 128), 128)
        held, came = w_ref[rows, :].astype(F32), w_in[rows, :].astype(F32)
        first = jnp.where(xh == 0, held, came)
        second = jnp.where(xh == 0, came, held)
        empty = jnp.zeros((128, 256), F32)
        wide = jnp.concatenate([first, empty], axis=1) + pltpu.roll(
            jnp.concatenate([second, empty], axis=1), 224, 1
        )
        w1[rows, :] = wide.astype(BF16)
        w2[rows, :] = pltpu.roll(wide, 64, 1).astype(BF16)
        return carry

    lax.fori_loop(0, 8, widen, 0)

    def finish(h, carry):
        rows = pl.ds(pl.multiple_of(h * 128, 128), 128)
        mean = acc[rows, :] / jnp.sum(total[rows, :], axis=1, keepdims=True)
        att[z, core, :, rows] = jnp.dot(
            mean.astype(BF16), uv_ref[h], preferred_element_type=F32
        ).astype(BF16)
        return carry

    lax.fori_loop(0, 8, finish, 0)

    def multiply(zz):
        wait(att.at[zz, 1 - core], as_recv.at[zz])
        a = jnp.dot(att[zz, 0], w1[...], preferred_element_type=F32)
        b = jnp.dot(att[zz, 1], w2[...], preferred_element_type=F32)
        part[zz, :, 0:384] = a[:, 0:384].astype(BF16)
        part[zz, :, 384:512] = (a[:, 384:512] + b[:, 0:128]).astype(BF16)
        part[zz, :, 512:896] = b[:, 128:512].astype(BF16)
        for step in range(1, 8):
            y_, xl_ = (y + step // 2) % 4, (xl + step) % 2
            rows = pl.ds(pl.multiple_of((y_ * 2 + xl_) * 16, 16), 16)
            send(
                part.at[zz, rows], got.at[zz, head], c_send.at[0], c_recv.at[zz],
                at(z, xh, core, y_, xl_),
            )
        rows = pl.ds(pl.multiple_of(head * 16, 16), 16)
        got[zz, head] = part[zz, rows, :]

    def reduce(zz):
        wait(got.at[zz, 0:7], c_recv.at[zz])
        whole = got[zz, 0].astype(F32)
        for h in range(1, 8):
            whole = whole + got[zz, h].astype(F32)

        @pl.when(zz == z)
        def _():
            turned[z] = whole.astype(BF16)

        @pl.when(zz != z)
        def _():
            summed[zz] = whole.astype(BF16)
            send(
                summed.at[zz], turned.at[z], t_send.at[0], t_recv.at[z],
                at(zz, xh, core, y, xl),
            )

    def deliver(zz):
        @pl.when(zz != z)
        def _():
            wait(turned.at[zz], t_recv.at[zz])

        for c in range(2):
            window = slice(384 * c, 384 * c + 512)
            own = (zz == head) & (core == c)

            @pl.when(own)
            def _():
                final[head * 2 + core] = turned[zz, :, window]

            @pl.when(jnp.logical_not(own))
            def _():
                send(
                    turned.at[zz, :, window], final.at[head * 2 + core],
                    f_send.at[0], f_recv.at[0], at(z, xh, c, zz // 2, zz % 2),
                )

    def pair(s, work):
        def one(i, c):
            work(jnp.where(i == 0, (z + 8 - s) % 8, (z + s) % 8))
            return c

        lax.fori_loop(0, jnp.where((s >= 1) & (s <= 3), 2, 1), one, 0)

    def output_step(s, carry):
        @pl.when(s <= 4)
        def _():
            ring(att, s, 0, az_send, az_recv, as_send, as_recv)
            ring(att, s, 1, az_send, az_recv, as_send, as_recv)
            pair(s, multiply)

        @pl.when((s >= 1) & (s <= 5))
        def _():
            pair(s - 1, reduce)

        @pl.when(s >= 2)
        def _():
            pair(s - 2, deliver)

        return carry

    lax.fori_loop(0, 7, output_step, 0)

    wait(final.at[0:15], f_recv.at[0])
    for c in range(2):

        @pl.when(core == c)
        def _():
            def place(h, carry):
                rows = pl.ds(pl.multiple_of(h * 16, 16), 16)
                v0, v1 = final[h * 2].astype(F32), final[h * 2 + 1].astype(F32)
                empty = jnp.zeros((16, 512), F32)
                v0 = jnp.concatenate([v0, empty], axis=1)
                v1 = jnp.concatenate([v1, empty], axis=1)
                back = 64 * c
                column = lax.broadcasted_iota(jnp.int32, (16, 1024), 1)

                def turn(v, by):
                    return v if by % 1024 == 0 else pltpu.roll(v, by % 1024, 1)

                full = jnp.where(
                    column < 448,
                    jnp.where(column < 224, turn(v0, -back), turn(v1, 224 - back)),
                    jnp.where(column < 672, turn(v0, 224 - back), turn(v1, 448 - back)),
                )
                out_ref[rows, :] = full[:, 0:896].astype(BF16)
                return carry

            lax.fori_loop(0, 8, place, 0)

    wait(mine, x_sem.at[0])
    wait(w_in, w_sem.at[0])
    wait(lat.at[0:7, 0], lz_send.at[0])
    wait(lat.at[0:8, 0], ls_send.at[0])
    wait(att.at[0:7, 0], az_send.at[0])
    wait(att.at[0:8, 0], as_send.at[0])
    wait(part.at[0:7], c_send.at[0])
    wait(summed.at[0:7], t_send.at[0])
    wait(final.at[0:15], f_send.at[0])


def shards(queries, latent, key_rope, up_keys, up_values, out_weight, block_order):
    q = jnp.pad(jnp.transpose(queries, (1, 0, 2)), ((0, 0), (0, 0), (0, 64)))
    uk = jnp.transpose(up_keys, (1, 0, 2))
    uv = jnp.transpose(up_values, (1, 0, 2))
    w = jnp.pad(out_weight, ((0, 0), (0, 32)))
    rope = jnp.pad(key_rope, ((0, 0), (0, 64)))
    vmem = pl.BlockSpec(memory_space=pltpu.VMEM)
    smem = pl.BlockSpec(memory_space=pltpu.SMEM)
    dma = pltpu.SemaphoreType.DMA
    return pl.pallas_call(
        kernel,
        out_shape=jax.ShapeDtypeStruct((128, 896), BF16),
        in_specs=[vmem] * 6 + [smem],
        out_specs=vmem,
        scratch_shapes=[
            pltpu.VMEM((8, 2, 2, 144, 512), BF16),
            pltpu.VMEM((512, 640), BF16),
            pltpu.VMEM((1024, 640), BF16),
            pltpu.VMEM((128, 512), F32),
            pltpu.VMEM((1024, 512), F32),
            pltpu.VMEM((1024, 128), F32),
            pltpu.VMEM((1024, 128), F32),
            pltpu.VMEM((1024, 256), BF16),
            pltpu.VMEM((1024, 512), BF16),
            pltpu.VMEM((1024, 512), BF16),
            pltpu.VMEM((8, 2, 128, 1024), BF16),
            pltpu.VMEM((8, 128, 896), BF16),
            pltpu.VMEM((8, 8, 16, 896), BF16),
            pltpu.VMEM((8, 16, 896), BF16),
            pltpu.VMEM((8, 16, 896), BF16),
            pltpu.VMEM((16, 16, 512), BF16),
            dma((2,)), dma((2,)),
            dma((1,)), dma((8,)), dma((1,)), dma((8,)),
            dma((1,)), dma((8,)), dma((1,)), dma((8,)),
            dma((1,)), dma((8,)),
            dma((1,)), dma((8,)),
            dma((1,)), dma((1,)),
        ],
        compiler_params=pltpu.CompilerParams(
            collective_id=0, has_side_effects=True, vmem_limit_bytes=56 * 2**20
        ),
        cost_estimate=pl.CostEstimate(
            flops=25 * 10**9, bytes_accessed=4 * 2**20, transcendentals=4 * 2**20
        ),
        name="latent_attention",
    )(q, latent, rope, uk, uv, w, block_order)


def solution(mesh):
    placed = (
        P("ctx", "head", None),
        P("ctx", None),
        P("ctx", None),
        P(None, "head", None),
        P(None, "head", None),
        P("head", "ctx"),
        P(),
    )
    return jax.shard_map(
        shards, mesh=mesh, in_specs=placed, out_specs=P("ctx", "head"), check_vma=False
    )
```

```python
import functools

import jax
import jax.numpy as jnp
from jax import lax
from jax.experimental import pallas as pl
from jax.experimental.pallas import tpu as pltpu
from jax.sharding import PartitionSpec as P

MESH = pl.DeviceIdType.MESH
F32 = jnp.float32
BF16 = jnp.bfloat16
NT = (((1,), (1,)), ((), ()))
LOW = -1e30


def wait(ref, sem):
    pltpu.make_async_copy(ref, ref, sem).wait()


def kernel(
    q_hbm, lat_ref, rope_ref, uk_hbm, uv_hbm, w_hbm, order_ref, out_ref,
    lat, keys, qp, bias, acc, top, total, q_in, uk_in, uv_in, uk, uv, w, att, part, got, summed,
    turned, final,
    in_sem, x_sem, w_sem, lz_send, lz_recv, ly_send, ly_recv, ls_send, ls_recv,
    az_send, az_recv, as_send, as_recv, c_send, c_recv, t_send, t_recv, f_send, f_recv,
):
    ctx, head = lax.axis_index("ctx"), lax.axis_index("head")
    z, xh, core = ctx // 4, (ctx // 2) % 2, ctx % 2
    y, xl = head // 2, head % 2
    factor = (192.0 ** -0.5) * 1.4426950408889634

    def at(z_, xh_, core_, y_, xl_):
        return (z_ * 4 + xh_ * 2 + core_, y_ * 2 + xl_)

    sibling = at(z, xh, 1 - core, y, xl)
    x_next = at(z, 1 - xh, core, y, 1 - xl)
    x_far = at(z, 1 - xh, core, y, xl)

    def send(src, dst, send_sem, recv_sem, device):
        pltpu.make_async_remote_copy(
            src_ref=src, dst_ref=dst, send_sem=send_sem, recv_sem=recv_sem,
            device_id=device, device_id_type=MESH,
        ).start()

    def other_head(step, core_):
        return at(z, xh, core_, (y + step // 2) % 4, (xl + step) % 2)

    barrier = pltpu.get_barrier_semaphore()
    partners = [sibling, x_next, x_far]
    partners += [at((z + step) % 8, xh, core, y, xl) for step in range(1, 8)]
    partners += [other_head(step, c) for step in range(1, 8) for c in (core, 1 - core)]
    for device in partners:
        pl.semaphore_signal(barrier, inc=1, device_id=device, device_id_type=MESH)

    my_w = w.at[pl.ds(pl.multiple_of(64 + 224 * xh, 16), 224)]
    loads = [
        pltpu.make_async_copy(src, dst, in_sem.at[i])
        for i, (src, dst) in enumerate(
            [(q_hbm, q_in), (uk_hbm, uk_in), (uv_hbm, uv_in), (w_hbm, my_w)]
        )
    ]
    for load in loads:
        load.start()

    lat[z, core, xh, 0:128, :] = lat_ref[...]
    rope = jnp.concatenate([rope_ref[...].astype(F32), jnp.zeros((64, 128), F32)], axis=0).T
    rope = rope[0:64, :] + pltpu.roll(rope[64:128, :], 64, 1)
    for g in range(4):
        lat[z, core, xh, 128:144, g * 128 : (g + 1) * 128] = rope[g * 16 : (g + 1) * 16, :].astype(BF16)

    pl.semaphore_wait(barrier, len(partners))
    mine = lat.at[z, core, xh]
    send(mine, mine, x_sem.at[0], x_sem.at[1], x_next)

    carried = (xh + y) % 2

    def ring(s, side):
        zz = (z + 8 - s) % 8 if side == 0 else (z + s) % 8
        block = lat.at[zz, core, carried]
        active = (s <= 4) if side == 0 else ((s >= 1) & (s <= 3))

        @pl.when(active & (s > 0))
        def _():
            wait(block, lz_recv.at[zz])

        @pl.when((s < 3) | ((s == 3) & (core == side)))
        def _():
            to = (z + 1) % 8 if side == 0 else (z + 7) % 8
            send(block, block, lz_send.at[0], lz_recv.at[zz], at(to, xh, core, y, xl))

        down = (s <= 3) | (core == 0) if side == 0 else (s < 0)

        @pl.when(active & (s > 0) & down)
        def _():
            send(block, block, ly_send.at[0], ly_recv.at[zz], at(z, xh, core, (y + 3) % 4, xl))

        @pl.when(active & (s > 0) & jnp.logical_not(down))
        def _():
            send(block, block, ly_send.at[0], ly_recv.at[zz], at(z, xh, core, (y + 1) % 4, xl))

        @pl.when(active)
        def _():
            send(block, block, ls_send.at[0], ls_recv.at[zz, carried], sibling)

    def across(zz):
        block = lat.at[zz, core, 1 - carried]

        @pl.when(zz != z)
        def _():
            wait(block, ly_recv.at[zz])

        send(block, block, ls_send.at[0], ls_recv.at[zz, 1 - carried], sibling)

    @pl.when(carried == xh)
    def _():
        ring(0, 0)
        ring(0, 1)

    wait(mine, x_sem.at[1])

    @pl.when(carried != xh)
    def _():
        ring(0, 0)
        ring(0, 1)

    across(z)
    for load in loads[3:]:
        load.wait()
    send(my_w, my_w, w_sem.at[0], w_sem.at[1], x_far)

    w[0:64, :] = jnp.zeros((64, 1024), BF16)
    w[512:576, :] = jnp.zeros((64, 1024), BF16)

    for load in loads[0:3]:
        load.wait()
    to_row = lax.broadcasted_iota(jnp.int32, (256, 256), 0)
    from_row = lax.broadcasted_iota(jnp.int32, (256, 256), 1)
    turn_rows = jnp.where(
        from_row == (to_row & 31) * 8 + (to_row >> 5), 1.0, 0.0
    ).astype(BF16)

    def by_head(i, carry):
        rows = pl.ds(pl.multiple_of(i * 256, 256), 256)
        both = jnp.concatenate([uk_in[rows, :], uv_in[rows, :]], axis=1)
        both = jnp.dot(turn_rows, both, preferred_element_type=F32).astype(BF16)
        held = pl.ds(pl.multiple_of(i * 32, 32), 32)
        for h in range(8):
            uk[h, held, :] = both[h * 32 : h * 32 + 32, 0:128]
            uv[h, held, :] = both[h * 32 : h * 32 + 32, 128:256]
        return carry

    lax.fori_loop(0, 16, by_head, 0)

    def project(h, carry):
        rows = pl.ds(pl.multiple_of(h * 128, 128), 128)
        q = q_in[h].astype(F32)
        plain = q[0:128, :].T.astype(BF16)
        qp[rows, 0:512] = lax.dot_general(
            plain, uk[h], NT, preferred_element_type=F32
        ).astype(BF16)
        turned_rope = jnp.concatenate([q[128:192, :], jnp.zeros((64, 128), F32)], axis=0).T
        qp[rows, 512:640] = turned_rope.astype(BF16)
        return carry

    lax.fori_loop(0, 8, project, 0)
    top[...] = jnp.full_like(top, LOW)
    total[...] = jnp.zeros_like(total)
    acc[...] = jnp.zeros_like(acc)

    lane = lax.broadcasted_iota(jnp.int32, (8, 512), 1)
    row = lax.broadcasted_iota(jnp.int32, (128, 512), 0)

    def attend(zz):
        for x in range(2):
            wait(lat.at[zz, 1 - core, x], ls_recv.at[zz, x])
        place = jnp.zeros((8, 512), jnp.int32)
        for c in range(2):
            for x in range(2):
                n = c * 2 + x
                for half in range(2):
                    block = order_ref[zz * 8 + x * 4 + c * 2 + half] * 64
                    place = jnp.where((lane >> 6) == n * 2 + half, block + (lane & 63), place)
                keys[n * 128 : (n + 1) * 128, 0:512] = lat[zz, c, x, 0:128, :]
                for g in range(4):
                    pair = lat[zz, c, x, 128:144, g * 128 : (g + 1) * 128]
                    keys[n * 128 + g * 16 : n * 128 + g * 16 + 16, 512:640] = pair
                    turn = pltpu.roll(pair.astype(F32), 64, 1).astype(BF16)
                    keys[n * 128 + 64 + g * 16 : n * 128 + 64 + g * 16 + 16, 512:640] = turn
        own = row + jnp.where(
            row < 64, order_ref[ctx * 2] * 64, order_ref[ctx * 2 + 1] * 64 - 64
        )
        bias[...] = jnp.where(place[0:1, :] <= own, 0.0, LOW)
        for r in range(2):
            rows = slice(r * 512, (r + 1) * 512)
            s = lax.dot_general(qp[rows, :], keys[...], NT, preferred_element_type=F32)
            s = s + jnp.concatenate([bias[...]] * 4, axis=0)
            old = top[rows, :]
            new = jnp.maximum(old, jnp.max(s, axis=1, keepdims=True))
            top[rows, :] = new
            p = jnp.exp2((s - jnp.concatenate([new] * 4, axis=1)) * factor)
            fade = jnp.exp2((old - new) * factor)
            total[rows, :] = total[rows, :] * fade + (
                (p[:, 0:128] + p[:, 128:256]) + (p[:, 256:384] + p[:, 384:512])
            )
            added = jnp.dot(p.astype(BF16), keys[:, 0:512], preferred_element_type=F32)
            acc[rows, :] = acc[rows, :] * jnp.concatenate([fade] * 4, axis=1) + added

    def pair(s, work):
        def one(i, c):
            work(jnp.where(i == 0, (z + 8 - s) % 8, (z + s) % 8))
            return c

        lax.fori_loop(0, jnp.where((s >= 1) & (s <= 3), 2, 1), one, 0)

    def gather_step(s, carry):
        @pl.when((s >= 1) & (s <= 4))
        def _():
            ring(s, 0)
            ring(s, 1)

        @pl.when(s >= 2)
        def _():
            pair(s - 1, across)

        @pl.when(s >= 1)
        def _():
            pair(s - 1, attend)

        return carry

    lax.fori_loop(1, 6, gather_step, 0)
    wait(my_w, w_sem.at[1])

    def att_ring(s, side, u):
        zz = (z + 8 - s) % 8 if side == 0 else (z + s) % 8
        block = att.at[zz, core, u]
        active = (s >= 0) if side == 0 else ((s >= 1) & (s <= 3))

        @pl.when(active & (s > 0))
        def _():
            wait(block, az_recv.at[zz, u])

        @pl.when((s < 3) | ((s == 3) & (core == side)))
        def _():
            to = (z + 1) % 8 if side == 0 else (z + 7) % 8
            send(block, block, az_send.at[0], az_recv.at[zz, u], at(to, xh, core, y, xl))

        @pl.when(active)
        def _():
            send(block, block, as_send.at[0], as_recv.at[zz, u], sibling)

    for u in range(2):
        for v in range(4):
            h = u * 4 + v
            rows = slice(h * 128, h * 128 + 128)
            scale = 1.0 / jnp.sum(total[rows, :], axis=1, keepdims=True)
            att[z, core, u, :, v * 128 : v * 128 + 128] = jnp.dot(
                (acc[rows, :] * scale).astype(BF16), uv[h], preferred_element_type=F32
            ).astype(BF16)
        att_ring(0, 0, u)
        att_ring(0, 1, u)

    def multiply(zz):
        for u in range(2):
            wait(att.at[zz, 1 - core, u], as_recv.at[zz, u])

        def product(c, rows):
            return sum(
                lax.dot_general(
                    att[zz, c, u], w[rows, u * 512 : u * 512 + 512], NT, preferred_element_type=F32
                )
                for u in range(2)
            )

        a = product(0, slice(64, 576))
        b = product(1, slice(0, 512))
        part[zz, :, 0:384] = a[:, 0:384].astype(BF16)
        part[zz, :, 384:512] = (a[:, 384:512] + b[:, 0:128]).astype(BF16)
        part[zz, :, 512:896] = b[:, 128:512].astype(BF16)
        for step in range(1, 8):
            y_, xl_ = (y + step // 2) % 4, (xl + step) % 2
            rows = pl.ds(pl.multiple_of((y_ * 2 + xl_) * 16, 16), 16)
            send(
                part.at[zz, rows], got.at[zz, head], c_send.at[0], c_recv.at[zz],
                at(z, xh, core, y_, xl_),
            )
        rows = pl.ds(pl.multiple_of(head * 16, 16), 16)
        got[zz, head] = part[zz, rows, :]

    def reduce(zz):
        wait(got.at[zz, 0:7], c_recv.at[zz])
        whole = got[zz, 0].astype(F32)
        for h in range(1, 8):
            whole = whole + got[zz, h].astype(F32)

        @pl.when(zz == z)
        def _():
            turned[z] = whole.astype(BF16)

        @pl.when(zz != z)
        def _():
            summed[zz] = whole.astype(BF16)
            send(
                summed.at[zz], turned.at[z], t_send.at[0], t_recv.at[z],
                at(zz, xh, core, y, xl),
            )

    def deliver(zz):
        @pl.when(zz != z)
        def _():
            wait(turned.at[zz], t_recv.at[zz])

        for c in range(2):
            window = slice(384 * c, 384 * c + 512)
            own = (zz == head) & (core == c)

            @pl.when(own)
            def _():
                final[head * 2 + core] = turned[zz, :, window]

            @pl.when(jnp.logical_not(own))
            def _():
                send(
                    turned.at[zz, :, window], final.at[head * 2 + core],
                    f_send.at[0], f_recv.at[0], at(z, xh, c, zz // 2, zz % 2),
                )

    def output_step(s, carry):
        @pl.when((s >= 1) & (s <= 4))
        def _():
            for u in range(2):
                att_ring(s, 0, u)
                att_ring(s, 1, u)

        @pl.when(s <= 4)
        def _():
            pair(s, multiply)

        @pl.when((s >= 1) & (s <= 5))
        def _():
            pair(s - 1, reduce)

        @pl.when(s >= 2)
        def _():
            pair(s - 2, deliver)

        return carry

    lax.fori_loop(0, 7, output_step, 0)

    wait(final.at[0:15], f_recv.at[0])
    for c in range(2):

        @pl.when(core == c)
        def _():
            def place(h, carry):
                rows = pl.ds(pl.multiple_of(h * 16, 16), 16)
                v0, v1 = final[h * 2].astype(F32), final[h * 2 + 1].astype(F32)
                empty = jnp.zeros((16, 512), F32)
                v0 = jnp.concatenate([v0, empty], axis=1)
                v1 = jnp.concatenate([v1, empty], axis=1)
                back = 64 * c
                column = lax.broadcasted_iota(jnp.int32, (16, 1024), 1)

                def turn(v, by):
                    return v if by % 1024 == 0 else pltpu.roll(v, by % 1024, 1)

                full = jnp.where(
                    column < 448,
                    jnp.where(column < 224, turn(v0, -back), turn(v1, 224 - back)),
                    jnp.where(column < 672, turn(v0, 224 - back), turn(v1, 448 - back)),
                )
                out_ref[rows, :] = full[:, 0:896].astype(BF16)
                return carry

            lax.fori_loop(0, 8, place, 0)

    wait(mine, x_sem.at[0])
    wait(my_w, w_sem.at[0])
    wait(lat.at[0:7, 0, 0], lz_send.at[0])
    wait(lat.at[0:7, 0, 0], ly_send.at[0])
    wait(lat.at[0:8, 0], ls_send.at[0])
    wait(att.at[0:7, 0], az_send.at[0])
    wait(att.at[0:8, 0], as_send.at[0])
    wait(part.at[0:7], c_send.at[0])
    wait(summed.at[0:7], t_send.at[0])
    wait(final.at[0:15], f_send.at[0])


def shards(queries, latent, key_rope, up_keys, up_values, out_weight, block_order):
    q = jnp.transpose(queries, (1, 2, 0))
    rope = jnp.transpose(key_rope)
    uk = up_keys.reshape(4096, 128)
    uv = up_values.reshape(4096, 128)
    w = jnp.transpose(out_weight)
    vmem = pl.BlockSpec(memory_space=pltpu.VMEM)
    hbm = pl.BlockSpec(memory_space=pl.ANY)
    smem = pl.BlockSpec(memory_space=pltpu.SMEM)
    dma = pltpu.SemaphoreType.DMA
    return pl.pallas_call(
        kernel,
        out_shape=jax.ShapeDtypeStruct((128, 896), BF16),
        in_specs=[hbm, vmem, vmem, hbm, hbm, hbm, smem],
        out_specs=vmem,
        scratch_shapes=[
            pltpu.VMEM((8, 2, 2, 144, 512), BF16),
            pltpu.VMEM((512, 640), BF16),
            pltpu.VMEM((1024, 640), BF16),
            pltpu.VMEM((128, 512), F32),
            pltpu.VMEM((1024, 512), F32),
            pltpu.VMEM((1024, 128), F32),
            pltpu.VMEM((1024, 128), F32),
            pltpu.VMEM((8, 192, 128), BF16),
            pltpu.VMEM((4096, 128), BF16),
            pltpu.VMEM((4096, 128), BF16),
            pltpu.VMEM((8, 512, 128), BF16),
            pltpu.VMEM((8, 512, 128), BF16),
            pltpu.VMEM((576, 1024), BF16),
            pltpu.VMEM((8, 2, 2, 128, 512), BF16),
            pltpu.VMEM((8, 128, 896), BF16),
            pltpu.VMEM((8, 8, 16, 896), BF16),
            pltpu.VMEM((8, 16, 896), BF16),
            pltpu.VMEM((8, 16, 896), BF16),
            pltpu.VMEM((16, 16, 512), BF16),
            dma((4,)), dma((2,)), dma((2,)),
            dma((1,)), dma((8,)), dma((1,)), dma((8,)), dma((1,)), dma((8, 2)),
            dma((1,)), dma((8, 2)), dma((1,)), dma((8, 2)),
            dma((1,)), dma((8,)),
            dma((1,)), dma((8,)),
            dma((1,)), dma((1,)),
        ],
        compiler_params=pltpu.CompilerParams(
            collective_id=0, has_side_effects=True, vmem_limit_bytes=56 * 2**20
        ),
        cost_estimate=pl.CostEstimate(
            flops=25 * 10**9, bytes_accessed=4 * 2**20, transcendentals=4 * 2**20
        ),
        name="latent_attention",
    )(q, latent, rope, uk, uv, w, block_order)


def solution(mesh):
    placed = (
        P("ctx", "head", None),
        P("ctx", None),
        P("ctx", None),
        P(None, "head", None),
        P(None, "head", None),
        P("head", "ctx"),
        P(),
    )
    return jax.shard_map(
        shards, mesh=mesh, in_specs=placed, out_specs=P("ctx", "head"), check_vma=False
    )
```

```python
import functools

import jax
import jax.numpy as jnp
from jax import lax
from jax.experimental import pallas as pl
from jax.experimental.pallas import tpu as pltpu
from jax.sharding import PartitionSpec as P

MESH = pl.DeviceIdType.MESH
F32 = jnp.float32
BF16 = jnp.bfloat16
NT = (((1,), (1,)), ((), ()))
LOW = -1e30


def wait(ref, sem):
    pltpu.make_async_copy(ref, ref, sem).wait()


def kernel(
    q_hbm, lat_ref, rope_ref, uk_hbm, uv_hbm, w_hbm, order_ref, out_ref,
    lat, keys, qp, bias, acc, top, total, q_in, uk_in, uv_in, uk, uv, w, att, part, got, summed,
    turned, final,
    in_sem, x_sem, w_sem, lz_send, lz_recv, ly_send, ly_recv, ls_send, ls_recv,
    az_send, az_recv, as_send, as_recv, c_send, c_recv, t_send, t_recv, f_send, f_recv,
):
    ctx, head = lax.axis_index("ctx"), lax.axis_index("head")
    z, xh, core = ctx // 4, (ctx // 2) % 2, ctx % 2
    y, xl = head // 2, head % 2
    factor = (192.0 ** -0.5) * 1.4426950408889634

    def at(z_, xh_, core_, y_, xl_):
        return (z_ * 4 + xh_ * 2 + core_, y_ * 2 + xl_)

    sibling = at(z, xh, 1 - core, y, xl)
    x_next = at(z, 1 - xh, core, y, 1 - xl)
    x_far = at(z, 1 - xh, core, y, xl)

    def send(src, dst, send_sem, recv_sem, device):
        pltpu.make_async_remote_copy(
            src_ref=src, dst_ref=dst, send_sem=send_sem, recv_sem=recv_sem,
            device_id=device, device_id_type=MESH,
        ).start()

    def other_head(step, core_):
        return at(z, xh, core_, (y + step // 2) % 4, (xl + step) % 2)

    barrier = pltpu.get_barrier_semaphore()
    partners = [sibling, x_next, x_far]
    partners += [at((z + step) % 8, xh, core, y, xl) for step in range(1, 8)]
    partners += [other_head(step, c) for step in range(1, 8) for c in (core, 1 - core)]
    for device in partners:
        pl.semaphore_signal(barrier, inc=1, device_id=device, device_id_type=MESH)

    my_w = w.at[pl.ds(pl.multiple_of(64 + 224 * xh, 16), 224)]
    loads = [
        pltpu.make_async_copy(src, dst, in_sem.at[i])
        for i, (src, dst) in enumerate(
            [(q_hbm, q_in), (uk_hbm, uk_in), (uv_hbm, uv_in), (w_hbm, my_w)]
        )
    ]
    for load in loads:
        load.start()

    lat[z, core, xh, 0:128, :] = lat_ref[...]
    rope = jnp.concatenate([rope_ref[...].astype(F32), jnp.zeros((64, 128), F32)], axis=0).T
    rope = rope[0:64, :] + pltpu.roll(rope[64:128, :], 64, 1)
    for g in range(4):
        lat[z, core, xh, 128:144, g * 128 : (g + 1) * 128] = rope[g * 16 : (g + 1) * 16, :].astype(BF16)

    pl.semaphore_wait(barrier, len(partners))
    mine = lat.at[z, core, xh]
    send(mine, mine, x_sem.at[0], x_sem.at[1], x_next)

    carried = (xh + y) % 2

    def ring(s, side):
        zz = (z + 8 - s) % 8 if side == 0 else (z + s) % 8
        block = lat.at[zz, core, carried]
        active = (s <= 4) if side == 0 else ((s >= 1) & (s <= 3))

        @pl.when(active & (s > 0))
        def _():
            wait(block, lz_recv.at[zz])

        @pl.when((s < 3) | ((s == 3) & (core == side)))
        def _():
            to = (z + 1) % 8 if side == 0 else (z + 7) % 8
            send(block, block, lz_send.at[0], lz_recv.at[zz], at(to, xh, core, y, xl))

        down = (s <= 3) | (core == 0) if side == 0 else (s < 0)

        @pl.when(active & (s > 0) & down)
        def _():
            send(block, block, ly_send.at[0], ly_recv.at[zz], at(z, xh, core, (y + 3) % 4, xl))

        @pl.when(active & (s > 0) & jnp.logical_not(down))
        def _():
            send(block, block, ly_send.at[0], ly_recv.at[zz], at(z, xh, core, (y + 1) % 4, xl))

        @pl.when(active)
        def _():
            send(block, block, ls_send.at[0], ls_recv.at[zz, carried], sibling)

    def across(zz):
        block = lat.at[zz, core, 1 - carried]

        @pl.when(zz != z)
        def _():
            wait(block, ly_recv.at[zz])

        send(block, block, ls_send.at[0], ls_recv.at[zz, 1 - carried], sibling)

    @pl.when(carried == xh)
    def _():
        ring(0, 0)
        ring(0, 1)

    wait(mine, x_sem.at[1])

    @pl.when(carried != xh)
    def _():
        ring(0, 0)
        ring(0, 1)

    across(z)
    for load in loads[3:]:
        load.wait()
    send(my_w, my_w, w_sem.at[0], w_sem.at[1], x_far)

    w[0:64, :] = jnp.zeros((64, 1024), BF16)
    w[512:576, :] = jnp.zeros((64, 1024), BF16)

    for load in loads[0:3]:
        load.wait()
    to_row = lax.broadcasted_iota(jnp.int32, (256, 256), 0)
    from_row = lax.broadcasted_iota(jnp.int32, (256, 256), 1)
    turn_rows = jnp.where(
        from_row == (to_row & 31) * 8 + (to_row >> 5), 1.0, 0.0
    ).astype(BF16)

    def by_head(i, carry):
        rows = pl.ds(pl.multiple_of(i * 256, 256), 256)
        both = jnp.concatenate([uk_in[rows, :], uv_in[rows, :]], axis=1)
        both = jnp.dot(turn_rows, both, preferred_element_type=F32).astype(BF16)
        held = pl.ds(pl.multiple_of(i * 32, 32), 32)
        for h in range(8):
            uk[h, held, :] = both[h * 32 : h * 32 + 32, 0:128]
            uv[h, held, :] = both[h * 32 : h * 32 + 32, 128:256]
        return carry

    lax.fori_loop(0, 16, by_head, 0)

    def project(h, carry):
        rows = pl.ds(pl.multiple_of(h * 128, 128), 128)
        q = q_in[h].astype(F32)
        plain = q[0:128, :].T.astype(BF16)
        qp[rows, 0:512] = lax.dot_general(
            plain, uk[h], NT, preferred_element_type=F32
        ).astype(BF16)
        turned_rope = jnp.concatenate([q[128:192, :], jnp.zeros((64, 128), F32)], axis=0).T
        qp[rows, 512:640] = turned_rope.astype(BF16)
        return carry

    lax.fori_loop(0, 8, project, 0)
    top[...] = jnp.full_like(top, LOW)
    total[...] = jnp.zeros_like(total)
    acc[...] = jnp.zeros_like(acc)

    lane = lax.broadcasted_iota(jnp.int32, (8, 512), 1)
    row = lax.broadcasted_iota(jnp.int32, (128, 512), 0)

    def load_keys(zz, slot):
        for x in range(2):
            wait(lat.at[zz, 1 - core, x], ls_recv.at[zz, x])
        place = jnp.zeros((8, 512), jnp.int32)
        for c in range(2):
            for x in range(2):
                n = c * 2 + x
                for half in range(2):
                    block = order_ref[zz * 8 + x * 4 + c * 2 + half] * 64
                    place = jnp.where((lane >> 6) == n * 2 + half, block + (lane & 63), place)
                keys[slot, n * 128 : (n + 1) * 128, 0:512] = lat[zz, c, x, 0:128, :]
                for g in range(4):
                    pair = lat[zz, c, x, 128:144, g * 128 : (g + 1) * 128]
                    keys[slot, n * 128 + g * 16 : n * 128 + g * 16 + 16, 512:640] = pair
                    turn = pltpu.roll(pair.astype(F32), 64, 1).astype(BF16)
                    keys[slot, n * 128 + 64 + g * 16 : n * 128 + 64 + g * 16 + 16, 512:640] = turn
        own = row + jnp.where(
            row < 64, order_ref[ctx * 2] * 64, order_ref[ctx * 2 + 1] * 64 - 64
        )
        bias[slot] = jnp.where(place[0:1, :] <= own, 0.0, LOW)

    def fold(slot, first, count):
        rows = slice(first * 512, (first + count) * 512)
        s = lax.dot_general(qp[rows, :], keys[slot], NT, preferred_element_type=F32)
        s = s + jnp.concatenate([bias[slot]] * (4 * count), axis=0)
        old = top[rows, :]
        new = jnp.maximum(old, jnp.max(s, axis=1, keepdims=True))
        top[rows, :] = new
        p = jnp.exp2((s - jnp.concatenate([new] * 4, axis=1)) * factor)
        fade = jnp.exp2((old - new) * factor)
        total[rows, :] = total[rows, :] * fade + (
            (p[:, 0:128] + p[:, 128:256]) + (p[:, 256:384] + p[:, 384:512])
        )
        added = jnp.dot(p.astype(BF16), keys[slot, :, 0:512], preferred_element_type=F32)
        acc[rows, :] = acc[rows, :] * jnp.concatenate([fade] * 4, axis=1) + added

    def attend(zz):
        load_keys(zz, 0)
        fold(0, 0, 2)

    def pair(s, work):
        def one(i, c):
            work(jnp.where(i == 0, (z + 8 - s) % 8, (z + s) % 8))
            return c

        lax.fori_loop(0, jnp.where((s >= 1) & (s <= 3), 2, 1), one, 0)

    def gather_step(s, carry):
        @pl.when(s >= 2)
        def _():
            pair(s - 1, across)

        ring(s, 0)
        ring(s, 1)

        @pl.when(s <= 3)
        def _():
            pair(s - 1, attend)

        return carry

    lax.fori_loop(1, 5, gather_step, 0)

    def att_ring(s, side, u):
        zz = (z + 8 - s) % 8 if side == 0 else (z + s) % 8
        block = att.at[zz, core, u]
        active = (s >= 0) if side == 0 else ((s >= 1) & (s <= 3))

        @pl.when(active & (s > 0))
        def _():
            wait(block, az_recv.at[zz, u])

        @pl.when((s < 3) | ((s == 3) & (core == side)))
        def _():
            to = (z + 1) % 8 if side == 0 else (z + 7) % 8
            send(block, block, az_send.at[0], az_recv.at[zz, u], at(to, xh, core, y, xl))

        @pl.when(active)
        def _():
            send(block, block, as_send.at[0], as_recv.at[zz, u], sibling)

    def finish(u):
        for v in range(4):
            h = u * 4 + v
            rows = slice(h * 128, h * 128 + 128)
            scale = 1.0 / jnp.sum(total[rows, :], axis=1, keepdims=True)
            att[z, core, u, :, v * 128 : v * 128 + 128] = jnp.dot(
                (acc[rows, :] * scale).astype(BF16), uv[h], preferred_element_type=F32
            ).astype(BF16)
        att_ring(0, 0, u)
        att_ring(0, 1, u)

    load_keys((z + 5) % 8, 0)
    load_keys((z + 3) % 8, 1)
    fold(0, 0, 1)
    fold(1, 0, 1)
    across((z + 4) % 8)
    load_keys((z + 4) % 8, 2)
    fold(2, 0, 1)
    finish(0)
    for slot in range(3):
        fold(slot, 1, 1)
    finish(1)
    wait(my_w, w_sem.at[1])

    def multiply(zz):
        for u in range(2):
            wait(att.at[zz, 1 - core, u], as_recv.at[zz, u])

        def product(c, rows):
            return sum(
                lax.dot_general(
                    att[zz, c, u], w[rows, u * 512 : u * 512 + 512], NT, preferred_element_type=F32
                )
                for u in range(2)
            )

        a = product(0, slice(64, 576))
        b = product(1, slice(0, 512))
        part[zz, :, 0:384] = a[:, 0:384].astype(BF16)
        part[zz, :, 384:512] = (a[:, 384:512] + b[:, 0:128]).astype(BF16)
        part[zz, :, 512:896] = b[:, 128:512].astype(BF16)
        for step in range(1, 8):
            y_, xl_ = (y + step // 2) % 4, (xl + step) % 2
            rows = pl.ds(pl.multiple_of((y_ * 2 + xl_) * 16, 16), 16)
            send(
                part.at[zz, rows], got.at[zz, head], c_send.at[0], c_recv.at[zz],
                at(z, xh, core, y_, xl_),
            )
        rows = pl.ds(pl.multiple_of(head * 16, 16), 16)
        got[zz, head] = part[zz, rows, :]

    def reduce(zz):
        wait(got.at[zz, 0:7], c_recv.at[zz])
        whole = got[zz, 0].astype(F32)
        for h in range(1, 8):
            whole = whole + got[zz, h].astype(F32)

        @pl.when(zz == z)
        def _():
            turned[z] = whole.astype(BF16)

        @pl.when(zz != z)
        def _():
            summed[zz] = whole.astype(BF16)
            send(
                summed.at[zz], turned.at[z], t_send.at[0], t_recv.at[z],
                at(zz, xh, core, y, xl),
            )

    def deliver(zz):
        @pl.when(zz != z)
        def _():
            wait(turned.at[zz], t_recv.at[zz])

        for c in range(2):
            window = slice(384 * c, 384 * c + 512)
            own = (zz == head) & (core == c)

            @pl.when(own)
            def _():
                final[head * 2 + core] = turned[zz, :, window]

            @pl.when(jnp.logical_not(own))
            def _():
                send(
                    turned.at[zz, :, window], final.at[head * 2 + core],
                    f_send.at[0], f_recv.at[0], at(z, xh, c, zz // 2, zz % 2),
                )

    def output_step(s, carry):
        @pl.when((s >= 1) & (s <= 4))
        def _():
            for u in range(2):
                att_ring(s, 0, u)
                att_ring(s, 1, u)

        @pl.when(s <= 4)
        def _():
            pair(s, multiply)

        @pl.when((s >= 2) & (s <= 6))
        def _():
            pair(s - 2, reduce)

        @pl.when(s >= 3)
        def _():
            pair(s - 3, deliver)

        return carry

    lax.fori_loop(0, 8, output_step, 0)

    wait(final.at[0:15], f_recv.at[0])
    for c in range(2):

        @pl.when(core == c)
        def _():
            def place(h, carry):
                rows = pl.ds(pl.multiple_of(h * 16, 16), 16)
                v0, v1 = final[h * 2].astype(F32), final[h * 2 + 1].astype(F32)
                empty = jnp.zeros((16, 512), F32)
                v0 = jnp.concatenate([v0, empty], axis=1)
                v1 = jnp.concatenate([v1, empty], axis=1)
                back = 64 * c
                column = lax.broadcasted_iota(jnp.int32, (16, 1024), 1)

                def turn(v, by):
                    return v if by % 1024 == 0 else pltpu.roll(v, by % 1024, 1)

                full = jnp.where(
                    column < 448,
                    jnp.where(column < 224, turn(v0, -back), turn(v1, 224 - back)),
                    jnp.where(column < 672, turn(v0, 224 - back), turn(v1, 448 - back)),
                )
                out_ref[rows, :] = full[:, 0:896].astype(BF16)
                return carry

            lax.fori_loop(0, 8, place, 0)

    wait(mine, x_sem.at[0])
    wait(my_w, w_sem.at[0])
    wait(lat.at[0:7, 0, 0], lz_send.at[0])
    wait(lat.at[0:7, 0, 0], ly_send.at[0])
    wait(lat.at[0:8, 0], ls_send.at[0])
    wait(att.at[0:7, 0], az_send.at[0])
    wait(att.at[0:8, 0], as_send.at[0])
    wait(part.at[0:7], c_send.at[0])
    wait(summed.at[0:7], t_send.at[0])
    wait(final.at[0:15], f_send.at[0])


def shards(queries, latent, key_rope, up_keys, up_values, out_weight, block_order):
    q = jnp.transpose(queries, (1, 2, 0))
    rope = jnp.transpose(key_rope)
    uk = up_keys.reshape(4096, 128)
    uv = up_values.reshape(4096, 128)
    w = jnp.transpose(out_weight)
    vmem = pl.BlockSpec(memory_space=pltpu.VMEM)
    hbm = pl.BlockSpec(memory_space=pl.ANY)
    smem = pl.BlockSpec(memory_space=pltpu.SMEM)
    dma = pltpu.SemaphoreType.DMA
    return pl.pallas_call(
        kernel,
        out_shape=jax.ShapeDtypeStruct((128, 896), BF16),
        in_specs=[hbm, vmem, vmem, hbm, hbm, hbm, smem],
        out_specs=vmem,
        scratch_shapes=[
            pltpu.VMEM((8, 2, 2, 144, 512), BF16),
            pltpu.VMEM((3, 512, 640), BF16),
            pltpu.VMEM((1024, 640), BF16),
            pltpu.VMEM((3, 128, 512), F32),
            pltpu.VMEM((1024, 512), F32),
            pltpu.VMEM((1024, 128), F32),
            pltpu.VMEM((1024, 128), F32),
            pltpu.VMEM((8, 192, 128), BF16),
            pltpu.VMEM((4096, 128), BF16),
            pltpu.VMEM((4096, 128), BF16),
            pltpu.VMEM((8, 512, 128), BF16),
            pltpu.VMEM((8, 512, 128), BF16),
            pltpu.VMEM((576, 1024), BF16),
            pltpu.VMEM((8, 2, 2, 128, 512), BF16),
            pltpu.VMEM((8, 128, 896), BF16),
            pltpu.VMEM((8, 8, 16, 896), BF16),
            pltpu.VMEM((8, 16, 896), BF16),
            pltpu.VMEM((8, 16, 896), BF16),
            pltpu.VMEM((16, 16, 512), BF16),
            dma((4,)), dma((2,)), dma((2,)),
            dma((1,)), dma((8,)), dma((1,)), dma((8,)), dma((1,)), dma((8, 2)),
            dma((1,)), dma((8, 2)), dma((1,)), dma((8, 2)),
            dma((1,)), dma((8,)),
            dma((1,)), dma((8,)),
            dma((1,)), dma((1,)),
        ],
        compiler_params=pltpu.CompilerParams(
            collective_id=0, has_side_effects=True, vmem_limit_bytes=56 * 2**20
        ),
        cost_estimate=pl.CostEstimate(
            flops=25 * 10**9, bytes_accessed=4 * 2**20, transcendentals=4 * 2**20
        ),
        name="latent_attention",
    )(q, latent, rope, uk, uv, w, block_order)


def solution(mesh):
    placed = (
        P("ctx", "head", None),
        P("ctx", None),
        P("ctx", None),
        P(None, "head", None),
        P(None, "head", None),
        P("head", "ctx"),
        P(),
    )
    return jax.shard_map(
        shards, mesh=mesh, in_specs=placed, out_specs=P("ctx", "head"), check_vma=False
    )
```

```python
import functools

import jax
import jax.numpy as jnp
from jax import lax
from jax.experimental import pallas as pl
from jax.experimental.pallas import tpu as pltpu
from jax.sharding import PartitionSpec as P

MESH = pl.DeviceIdType.MESH
F32 = jnp.float32
BF16 = jnp.bfloat16
NT = (((1,), (1,)), ((), ()))
LOW = -1e30


def wait(ref, sem):
    pltpu.make_async_copy(ref, ref, sem).wait()


def kernel(
    q_hbm, lat_hbm, rope_hbm, uk_hbm, uv_hbm, w_hbm, order_hbm, out_ref,
    order_ref, rope_ref, lat, keys, qp, bias, acc, top, total, q_in, uk_in, uv_in, uk, uv, w, att, part, got, summed,
    turned, final,
    in_sem, x_sem, w_sem, lz_send, lz_recv, ly_send, ly_recv, ls_send, ls_recv,
    az_send, az_recv, as_send, as_recv, c_send, c_recv, t_send, t_recv, f_send, f_recv,
):
    ctx, head = lax.axis_index("ctx"), lax.axis_index("head")
    z, xh, core = ctx // 4, (ctx // 2) % 2, ctx % 2
    y, xl = head // 2, head % 2
    factor = (192.0 ** -0.5) * 1.4426950408889634

    def at(z_, xh_, core_, y_, xl_):
        return (z_ * 4 + xh_ * 2 + core_, y_ * 2 + xl_)

    sibling = at(z, xh, 1 - core, y, xl)
    x_next = at(z, 1 - xh, core, y, 1 - xl)
    x_far = at(z, 1 - xh, core, y, xl)

    def send(src, dst, send_sem, recv_sem, device):
        pltpu.make_async_remote_copy(
            src_ref=src, dst_ref=dst, send_sem=send_sem, recv_sem=recv_sem,
            device_id=device, device_id_type=MESH,
        ).start()

    def other_head(step, core_):
        return at(z, xh, core_, (y + step // 2) % 4, (xl + step) % 2)

    barrier = pltpu.get_barrier_semaphore()
    partners = [sibling, x_next, x_far]
    partners += [at((z + step) % 8, xh, core, y, xl) for step in range(1, 8)]
    partners += [other_head(step, c) for step in range(1, 8) for c in (core, 1 - core)]
    for device in partners:
        pl.semaphore_signal(barrier, inc=1, device_id=device, device_id_type=MESH)

    my_w = w.at[pl.ds(pl.multiple_of(64 + 224 * xh, 16), 224)]
    loads = [
        pltpu.make_async_copy(src, dst, in_sem.at[i])
        for i, (src, dst) in enumerate(
            [(q_hbm, q_in), (uk_hbm, uk_in), (uv_hbm, uv_in), (w_hbm, my_w)]
            + [(lat_hbm, lat.at[z, core, xh, 0:128]), (rope_hbm, rope_ref), (order_hbm, order_ref)]
        )
    ]
    for load in loads[4:] + loads[0:4]:
        load.start()

    for load in loads[4:]:
        load.wait()
    rope = jnp.concatenate([rope_ref[...].astype(F32), jnp.zeros((64, 128), F32)], axis=0).T
    rope = rope[0:64, :] + pltpu.roll(rope[64:128, :], 64, 1)
    for g in range(4):
        lat[z, core, xh, 128:144, g * 128 : (g + 1) * 128] = rope[g * 16 : (g + 1) * 16, :].astype(BF16)

    pl.semaphore_wait(barrier, len(partners))
    mine = lat.at[z, core, xh]
    send(mine, mine, x_sem.at[0], x_sem.at[1], x_next)

    carried = (xh + y) % 2

    def ring(s, side):
        zz = (z + 8 - s) % 8 if side == 0 else (z + s) % 8
        block = lat.at[zz, core, carried]
        active = (s <= 4) if side == 0 else ((s >= 1) & (s <= 3))

        @pl.when(active & (s > 0))
        def _():
            wait(block, lz_recv.at[zz])

        @pl.when((s < 3) | ((s == 3) & (core == side)))
        def _():
            to = (z + 1) % 8 if side == 0 else (z + 7) % 8
            send(block, block, lz_send.at[0], lz_recv.at[zz], at(to, xh, core, y, xl))

        down = (s <= 3) | (core == 0) if side == 0 else (s < 0)

        @pl.when(active & (s > 0) & down)
        def _():
            send(block, block, ly_send.at[0], ly_recv.at[zz], at(z, xh, core, (y + 3) % 4, xl))

        @pl.when(active & (s > 0) & jnp.logical_not(down))
        def _():
            send(block, block, ly_send.at[0], ly_recv.at[zz], at(z, xh, core, (y + 1) % 4, xl))

        @pl.when(active)
        def _():
            send(block, block, ls_send.at[0], ls_recv.at[zz, carried], sibling)

    def across(zz):
        block = lat.at[zz, core, 1 - carried]

        @pl.when(zz != z)
        def _():
            wait(block, ly_recv.at[zz])

        send(block, block, ls_send.at[0], ls_recv.at[zz, 1 - carried], sibling)

    @pl.when(carried == xh)
    def _():
        ring(0, 0)
        ring(0, 1)

    wait(mine, x_sem.at[1])

    @pl.when(carried != xh)
    def _():
        ring(0, 0)
        ring(0, 1)

    across(z)
    loads[3].wait()
    send(my_w, my_w, w_sem.at[0], w_sem.at[1], x_far)

    w[0:64, :] = jnp.zeros((64, 1024), BF16)
    w[512:576, :] = jnp.zeros((64, 1024), BF16)

    for load in loads[0:3]:
        load.wait()
    to_row = lax.broadcasted_iota(jnp.int32, (256, 256), 0)
    from_row = lax.broadcasted_iota(jnp.int32, (256, 256), 1)
    turn_rows = jnp.where(
        from_row == (to_row & 31) * 8 + (to_row >> 5), 1.0, 0.0
    ).astype(BF16)

    def by_head(i, carry):
        rows = pl.ds(pl.multiple_of(i * 256, 256), 256)
        both = jnp.concatenate([uk_in[rows, :], uv_in[rows, :]], axis=1)
        both = jnp.dot(turn_rows, both, preferred_element_type=F32).astype(BF16)
        held = pl.ds(pl.multiple_of(i * 32, 32), 32)
        for h in range(8):
            uk[h, held, :] = both[h * 32 : h * 32 + 32, 0:128]
            uv[h, held, :] = both[h * 32 : h * 32 + 32, 128:256]
        return carry

    lax.fori_loop(0, 16, by_head, 0)

    def project(h, carry):
        rows = pl.ds(pl.multiple_of(h * 128, 128), 128)
        q = q_in[h].astype(F32)
        plain = q[0:128, :].T.astype(BF16)
        qp[rows, 0:512] = lax.dot_general(
            plain, uk[h], NT, preferred_element_type=F32
        ).astype(BF16)
        turned_rope = jnp.concatenate([q[128:192, :], jnp.zeros((64, 128), F32)], axis=0).T
        qp[rows, 512:640] = turned_rope.astype(BF16)
        return carry

    lax.fori_loop(0, 8, project, 0)
    top[...] = jnp.full_like(top, LOW)
    total[...] = jnp.zeros_like(total)
    acc[...] = jnp.zeros_like(acc)

    lane = lax.broadcasted_iota(jnp.int32, (8, 512), 1)
    row = lax.broadcasted_iota(jnp.int32, (128, 512), 0)

    def load_keys(zz, slot):
        for x in range(2):
            wait(lat.at[zz, 1 - core, x], ls_recv.at[zz, x])
        place = jnp.zeros((8, 512), jnp.int32)
        for c in range(2):
            for x in range(2):
                n = c * 2 + x
                for half in range(2):
                    block = order_ref[zz * 8 + x * 4 + c * 2 + half] * 64
                    place = jnp.where((lane >> 6) == n * 2 + half, block + (lane & 63), place)
                keys[slot, n * 128 : (n + 1) * 128, 0:512] = lat[zz, c, x, 0:128, :]
                for g in range(4):
                    pair = lat[zz, c, x, 128:144, g * 128 : (g + 1) * 128]
                    keys[slot, n * 128 + g * 16 : n * 128 + g * 16 + 16, 512:640] = pair
                    turn = pltpu.roll(pair.astype(F32), 64, 1).astype(BF16)
                    keys[slot, n * 128 + 64 + g * 16 : n * 128 + 64 + g * 16 + 16, 512:640] = turn
        own = row + jnp.where(
            row < 64, order_ref[ctx * 2] * 64, order_ref[ctx * 2 + 1] * 64 - 64
        )
        bias[slot] = jnp.where(place[0:1, :] <= own, 0.0, LOW)

    def fold(slot, first, count):
        rows = slice(first * 512, (first + count) * 512)
        s = lax.dot_general(qp[rows, :], keys[slot], NT, preferred_element_type=F32)
        s = s + jnp.concatenate([bias[slot]] * (4 * count), axis=0)
        old = top[rows, :]
        new = jnp.maximum(old, jnp.max(s, axis=1, keepdims=True))
        top[rows, :] = new
        p = jnp.exp2((s - jnp.concatenate([new] * 4, axis=1)) * factor)
        fade = jnp.exp2((old - new) * factor)
        total[rows, :] = total[rows, :] * fade + (
            (p[:, 0:128] + p[:, 128:256]) + (p[:, 256:384] + p[:, 384:512])
        )
        added = jnp.dot(p.astype(BF16), keys[slot, :, 0:512], preferred_element_type=F32)
        acc[rows, :] = acc[rows, :] * jnp.concatenate([fade] * 4, axis=1) + added

    def attend(zz):
        load_keys(zz, 0)
        fold(0, 0, 2)

    def pair(s, work):
        def one(i, c):
            work(jnp.where(i == 0, (z + 8 - s) % 8, (z + s) % 8))
            return c

        lax.fori_loop(0, jnp.where((s >= 1) & (s <= 3), 2, 1), one, 0)

    def gather_step(s, carry):
        @pl.when(s >= 2)
        def _():
            pair(s - 1, across)

        ring(s, 0)
        ring(s, 1)

        @pl.when(s <= 3)
        def _():
            pair(s - 1, attend)

        return carry

    lax.fori_loop(1, 5, gather_step, 0)

    def att_ring(s, side, u):
        zz = (z + 8 - s) % 8 if side == 0 else (z + s) % 8
        block = att.at[zz, core, u]
        active = (s >= 0) if side == 0 else ((s >= 1) & (s <= 3))

        @pl.when(active & (s > 0))
        def _():
            wait(block, az_recv.at[zz, u])

        @pl.when((s < 3) | ((s == 3) & (core == side)))
        def _():
            to = (z + 1) % 8 if side == 0 else (z + 7) % 8
            send(block, block, az_send.at[0], az_recv.at[zz, u], at(to, xh, core, y, xl))

        @pl.when(active)
        def _():
            send(block, block, as_send.at[0], as_recv.at[zz, u], sibling)

    def finish(u):
        for v in range(4):
            h = u * 4 + v
            rows = slice(h * 128, h * 128 + 128)
            scale = 1.0 / jnp.sum(total[rows, :], axis=1, keepdims=True)
            att[z, core, u, :, v * 128 : v * 128 + 128] = jnp.dot(
                (acc[rows, :] * scale).astype(BF16), uv[h], preferred_element_type=F32
            ).astype(BF16)
        att_ring(0, 0, u)
        att_ring(0, 1, u)

    load_keys((z + 5) % 8, 0)
    load_keys((z + 3) % 8, 1)
    fold(0, 0, 1)
    fold(1, 0, 1)
    across((z + 4) % 8)
    load_keys((z + 4) % 8, 2)
    fold(2, 0, 1)
    finish(0)
    for slot in range(3):
        fold(slot, 1, 1)
    finish(1)
    wait(my_w, w_sem.at[1])

    def multiply(zz):
        for u in range(2):
            wait(att.at[zz, 1 - core, u], as_recv.at[zz, u])

        def product(c, rows):
            return sum(
                lax.dot_general(
                    att[zz, c, u], w[rows, u * 512 : u * 512 + 512], NT, preferred_element_type=F32
                )
                for u in range(2)
            )

        a = product(0, slice(64, 576))
        b = product(1, slice(0, 512))
        part[zz, :, 0:384] = a[:, 0:384].astype(BF16)
        part[zz, :, 384:512] = (a[:, 384:512] + b[:, 0:128]).astype(BF16)
        part[zz, :, 512:896] = b[:, 128:512].astype(BF16)
        for step in range(1, 8):
            y_, xl_ = (y + step // 2) % 4, (xl + step) % 2
            rows = pl.ds(pl.multiple_of((y_ * 2 + xl_) * 16, 16), 16)
            send(
                part.at[zz, rows], got.at[zz, head], c_send.at[0], c_recv.at[zz],
                at(z, xh, core, y_, xl_),
            )
        rows = pl.ds(pl.multiple_of(head * 16, 16), 16)
        got[zz, head] = part[zz, rows, :]

    def reduce(zz):
        wait(got.at[zz, 0:7], c_recv.at[zz])
        whole = got[zz, 0].astype(F32)
        for h in range(1, 8):
            whole = whole + got[zz, h].astype(F32)

        @pl.when(zz == z)
        def _():
            turned[z] = whole.astype(BF16)

        @pl.when(zz != z)
        def _():
            summed[zz] = whole.astype(BF16)
            send(
                summed.at[zz], turned.at[z], t_send.at[0], t_recv.at[z],
                at(zz, xh, core, y, xl),
            )

    def deliver(zz):
        @pl.when(zz != z)
        def _():
            wait(turned.at[zz], t_recv.at[zz])

        for c in range(2):
            window = slice(384 * c, 384 * c + 512)
            own = (zz == head) & (core == c)

            @pl.when(own)
            def _():
                final[head * 2 + core] = turned[zz, :, window]

            @pl.when(jnp.logical_not(own))
            def _():
                send(
                    turned.at[zz, :, window], final.at[head * 2 + core],
                    f_send.at[0], f_recv.at[0], at(z, xh, c, zz // 2, zz % 2),
                )

    def output_step(s, carry):
        @pl.when((s >= 1) & (s <= 4))
        def _():
            for u in range(2):
                att_ring(s, 0, u)
                att_ring(s, 1, u)

        @pl.when(s <= 4)
        def _():
            pair(s, multiply)

        @pl.when((s >= 2) & (s <= 6))
        def _():
            pair(s - 2, reduce)

        @pl.when(s >= 3)
        def _():
            pair(s - 3, deliver)

        return carry

    lax.fori_loop(0, 8, output_step, 0)

    wait(final.at[0:15], f_recv.at[0])
    for c in range(2):

        @pl.when(core == c)
        def _():
            def place(h, carry):
                rows = pl.ds(pl.multiple_of(h * 16, 16), 16)
                v0, v1 = final[h * 2].astype(F32), final[h * 2 + 1].astype(F32)
                empty = jnp.zeros((16, 512), F32)
                v0 = jnp.concatenate([v0, empty], axis=1)
                v1 = jnp.concatenate([v1, empty], axis=1)
                back = 64 * c
                column = lax.broadcasted_iota(jnp.int32, (16, 1024), 1)

                def turn(v, by):
                    return v if by % 1024 == 0 else pltpu.roll(v, by % 1024, 1)

                full = jnp.where(
                    column < 448,
                    jnp.where(column < 224, turn(v0, -back), turn(v1, 224 - back)),
                    jnp.where(column < 672, turn(v0, 224 - back), turn(v1, 448 - back)),
                )
                out_ref[rows, :] = full[:, 0:896].astype(BF16)
                return carry

            lax.fori_loop(0, 8, place, 0)

    wait(mine, x_sem.at[0])
    wait(my_w, w_sem.at[0])
    wait(lat.at[0:7, 0, 0], lz_send.at[0])
    wait(lat.at[0:7, 0, 0], ly_send.at[0])
    wait(lat.at[0:8, 0], ls_send.at[0])
    wait(att.at[0:7, 0], az_send.at[0])
    wait(att.at[0:8, 0], as_send.at[0])
    wait(part.at[0:7], c_send.at[0])
    wait(summed.at[0:7], t_send.at[0])
    wait(final.at[0:15], f_send.at[0])


def shards(queries, latent, key_rope, up_keys, up_values, out_weight, block_order):
    q = jnp.transpose(queries, (1, 2, 0))
    rope = jnp.transpose(key_rope)
    uk = up_keys.reshape(4096, 128)
    uv = up_values.reshape(4096, 128)
    w = jnp.transpose(out_weight)
    vmem = pl.BlockSpec(memory_space=pltpu.VMEM)
    hbm = pl.BlockSpec(memory_space=pl.ANY)
    dma = pltpu.SemaphoreType.DMA
    return pl.pallas_call(
        kernel,
        out_shape=jax.ShapeDtypeStruct((128, 896), BF16),
        in_specs=[hbm] * 7,
        out_specs=vmem,
        scratch_shapes=[
            pltpu.SMEM((64,), jnp.int32),
            pltpu.VMEM((64, 128), BF16),
            pltpu.VMEM((8, 2, 2, 144, 512), BF16),
            pltpu.VMEM((3, 512, 640), BF16),
            pltpu.VMEM((1024, 640), BF16),
            pltpu.VMEM((3, 128, 512), F32),
            pltpu.VMEM((1024, 512), F32),
            pltpu.VMEM((1024, 128), F32),
            pltpu.VMEM((1024, 128), F32),
            pltpu.VMEM((8, 192, 128), BF16),
            pltpu.VMEM((4096, 128), BF16),
            pltpu.VMEM((4096, 128), BF16),
            pltpu.VMEM((8, 512, 128), BF16),
            pltpu.VMEM((8, 512, 128), BF16),
            pltpu.VMEM((576, 1024), BF16),
            pltpu.VMEM((8, 2, 2, 128, 512), BF16),
            pltpu.VMEM((8, 128, 896), BF16),
            pltpu.VMEM((8, 8, 16, 896), BF16),
            pltpu.VMEM((8, 16, 896), BF16),
            pltpu.VMEM((8, 16, 896), BF16),
            pltpu.VMEM((16, 16, 512), BF16),
            dma((7,)), dma((2,)), dma((2,)),
            dma((1,)), dma((8,)), dma((1,)), dma((8,)), dma((1,)), dma((8, 2)),
            dma((1,)), dma((8, 2)), dma((1,)), dma((8, 2)),
            dma((1,)), dma((8,)),
            dma((1,)), dma((8,)),
            dma((1,)), dma((1,)),
        ],
        compiler_params=pltpu.CompilerParams(
            collective_id=0, has_side_effects=True, vmem_limit_bytes=56 * 2**20
        ),
        cost_estimate=pl.CostEstimate(
            flops=25 * 10**9, bytes_accessed=4 * 2**20, transcendentals=4 * 2**20
        ),
        name="latent_attention",
    )(q, latent, rope, uk, uv, w, block_order)


def solution(mesh):
    placed = (
        P("ctx", "head", None),
        P("ctx", None),
        P("ctx", None),
        P(None, "head", None),
        P(None, "head", None),
        P("head", "ctx"),
        P(),
    )
    return jax.shard_map(
        shards, mesh=mesh, in_specs=placed, out_specs=P("ctx", "head"), check_vma=False
    )
```

```python
import functools

import jax
import jax.numpy as jnp
from jax import lax
from jax.experimental import pallas as pl
from jax.experimental.pallas import tpu as pltpu
from jax.sharding import PartitionSpec as P

MESH = pl.DeviceIdType.MESH
F32 = jnp.float32
BF16 = jnp.bfloat16
NT = (((1,), (1,)), ((), ()))
LOW = -1e30


def wait(ref, sem):
    pltpu.make_async_copy(ref, ref, sem).wait()


def kernel(
    q_hbm, lat_hbm, rope_hbm, uk_hbm, uv_hbm, w_hbm, order_hbm, out_ref,
    order_ref, rope_ref, lat, keys, qp, bias, acc, top, total, q_in, uk_in, uv_in, uk, uv, w, att, part, got, summed,
    turned, final,
    in_sem, x_sem, w_sem, lz_send, lz_recv, ly_send, ly_recv, ls_send, ls_recv,
    az_send, az_recv, as_send, as_recv, c_send, c_recv, t_send, t_recv, f_send, f_recv,
):
    ctx, head = lax.axis_index("ctx"), lax.axis_index("head")
    z, xh, core = ctx // 4, (ctx // 2) % 2, ctx % 2
    y, xl = head // 2, head % 2
    factor = (192.0 ** -0.5) * 1.4426950408889634

    def at(z_, xh_, core_, y_, xl_):
        return (z_ * 4 + xh_ * 2 + core_, y_ * 2 + xl_)

    sibling = at(z, xh, 1 - core, y, xl)
    x_next = at(z, 1 - xh, core, y, 1 - xl)
    x_far = at(z, 1 - xh, core, y, xl)

    def send(src, dst, send_sem, recv_sem, device):
        pltpu.make_async_remote_copy(
            src_ref=src, dst_ref=dst, send_sem=send_sem, recv_sem=recv_sem,
            device_id=device, device_id_type=MESH,
        ).start()

    def other_head(step, core_):
        return at(z, xh, core_, (y + step // 2) % 4, (xl + step) % 2)

    barrier = pltpu.get_barrier_semaphore()
    partners = [sibling, x_next, x_far]
    partners += [at((z + step) % 8, xh, core, y, xl) for step in range(1, 8)]
    partners += [other_head(step, c) for step in range(1, 8) for c in (core, 1 - core)]
    for device in partners:
        pl.semaphore_signal(barrier, inc=1, device_id=device, device_id_type=MESH)

    my_w = w.at[pl.ds(pl.multiple_of(64 + 224 * xh, 16), 224)]
    loads = [
        pltpu.make_async_copy(src, dst, in_sem.at[i])
        for i, (src, dst) in enumerate(
            [(q_hbm, q_in), (uk_hbm, uk_in), (uv_hbm, uv_in), (w_hbm, my_w)]
            + [(lat_hbm, lat.at[z, core, xh, 0:128]), (rope_hbm, rope_ref), (order_hbm, order_ref)]
        )
    ]
    for load in loads[4:] + loads[0:4]:
        load.start()

    for load in loads[4:]:
        load.wait()
    rope = jnp.concatenate([rope_ref[...].astype(F32), jnp.zeros((64, 128), F32)], axis=0).T
    rope = rope[0:64, :] + pltpu.roll(rope[64:128, :], 64, 1)
    for g in range(4):
        lat[z, core, xh, 128:144, g * 128 : (g + 1) * 128] = rope[g * 16 : (g + 1) * 16, :].astype(BF16)

    pl.semaphore_wait(barrier, len(partners))
    mine = lat.at[z, core, xh]
    send(mine, mine, x_sem.at[0], x_sem.at[1], x_next)

    carried = (xh + y) % 2

    def ring(s, side):
        zz = (z + 8 - s) % 8 if side == 0 else (z + s) % 8
        block = lat.at[zz, core, carried]
        active = (s <= 4) if side == 0 else ((s >= 1) & (s <= 3))

        @pl.when(active & (s > 0))
        def _():
            wait(block, lz_recv.at[zz])

        @pl.when((s < 3) | ((s == 3) & (core == side)))
        def _():
            to = (z + 1) % 8 if side == 0 else (z + 7) % 8
            send(block, block, lz_send.at[0], lz_recv.at[zz], at(to, xh, core, y, xl))

        down = (s <= 3) | (core == 0) if side == 0 else (s < 0)

        @pl.when(active & (s > 0) & down)
        def _():
            send(block, block, ly_send.at[0], ly_recv.at[zz], at(z, xh, core, (y + 3) % 4, xl))

        @pl.when(active & (s > 0) & jnp.logical_not(down))
        def _():
            send(block, block, ly_send.at[0], ly_recv.at[zz], at(z, xh, core, (y + 1) % 4, xl))

        @pl.when(active)
        def _():
            send(block, block, ls_send.at[0], ls_recv.at[zz, carried], sibling)

    def across(zz):
        block = lat.at[zz, core, 1 - carried]

        @pl.when(zz != z)
        def _():
            wait(block, ly_recv.at[zz])

        send(block, block, ls_send.at[0], ls_recv.at[zz, 1 - carried], sibling)

    @pl.when(carried == xh)
    def _():
        ring(0, 0)
        ring(0, 1)

    wait(mine, x_sem.at[1])

    @pl.when(carried != xh)
    def _():
        ring(0, 0)
        ring(0, 1)

    across(z)
    loads[3].wait()
    send(my_w, my_w, w_sem.at[0], w_sem.at[1], x_far)

    w[0:64, :] = jnp.zeros((64, 1024), BF16)
    w[512:576, :] = jnp.zeros((64, 1024), BF16)

    for load in loads[0:3]:
        load.wait()
    to_row = lax.broadcasted_iota(jnp.int32, (256, 256), 0)
    from_row = lax.broadcasted_iota(jnp.int32, (256, 256), 1)
    turn_rows = jnp.where(
        from_row == (to_row & 31) * 8 + (to_row >> 5), 1.0, 0.0
    ).astype(BF16)

    def by_head(i, carry):
        rows = pl.ds(pl.multiple_of(i * 256, 256), 256)
        both = jnp.concatenate([uk_in[rows, :], uv_in[rows, :]], axis=1)
        both = jnp.dot(turn_rows, both, preferred_element_type=F32).astype(BF16)
        held = pl.ds(pl.multiple_of(i * 32, 32), 32)
        for h in range(8):
            uk[h, held, :] = both[h * 32 : h * 32 + 32, 0:128]
            uv[h, held, :] = both[h * 32 : h * 32 + 32, 128:256]
        return carry

    lax.fori_loop(0, 16, by_head, 0)

    def project(h, carry):
        rows = pl.ds(pl.multiple_of(h * 128, 128), 128)
        q = q_in[h].astype(F32)
        plain = q[0:128, :].T.astype(BF16)
        qp[rows, 0:512] = lax.dot_general(
            plain, uk[h], NT, preferred_element_type=F32
        ).astype(BF16)
        turned_rope = jnp.concatenate([q[128:192, :], jnp.zeros((64, 128), F32)], axis=0).T
        qp[rows, 512:640] = turned_rope.astype(BF16)
        return carry

    lax.fori_loop(0, 8, project, 0)
    top[...] = jnp.full_like(top, LOW)
    total[...] = jnp.zeros_like(total)
    acc[...] = jnp.zeros_like(acc)

    lane = lax.broadcasted_iota(jnp.int32, (8, 512), 1)
    row = lax.broadcasted_iota(jnp.int32, (128, 512), 0)

    def load_keys(zz, slot):
        for x in range(2):
            wait(lat.at[zz, 1 - core, x], ls_recv.at[zz, x])
        place = jnp.zeros((8, 512), jnp.int32)
        for c in range(2):
            for x in range(2):
                n = c * 2 + x
                for half in range(2):
                    block = order_ref[zz * 8 + x * 4 + c * 2 + half] * 64
                    place = jnp.where((lane >> 6) == n * 2 + half, block + (lane & 63), place)
                keys[slot, n * 128 : (n + 1) * 128, 0:512] = lat[zz, c, x, 0:128, :]
                for g in range(4):
                    pair = lat[zz, c, x, 128:144, g * 128 : (g + 1) * 128]
                    keys[slot, n * 128 + g * 16 : n * 128 + g * 16 + 16, 512:640] = pair
                    turn = pltpu.roll(pair.astype(F32), 64, 1).astype(BF16)
                    keys[slot, n * 128 + 64 + g * 16 : n * 128 + 64 + g * 16 + 16, 512:640] = turn
        own = row + jnp.where(
            row < 64, order_ref[ctx * 2] * 64, order_ref[ctx * 2 + 1] * 64 - 64
        )
        bias[slot] = jnp.where(place[0:1, :] <= own, 0.0, LOW)

    def fold(slot, first, count):
        rows = slice(first * 512, (first + count) * 512)
        s = lax.dot_general(qp[rows, :], keys[slot], NT, preferred_element_type=F32)
        s = s + jnp.concatenate([bias[slot]] * (4 * count), axis=0)
        old = top[rows, :]
        new = jnp.maximum(old, jnp.max(s, axis=1, keepdims=True))
        top[rows, :] = new
        p = jnp.exp2((s - jnp.concatenate([new] * 4, axis=1)) * factor)
        fade = jnp.exp2((old - new) * factor)
        total[rows, :] = total[rows, :] * fade + (
            (p[:, 0:128] + p[:, 128:256]) + (p[:, 256:384] + p[:, 384:512])
        )
        added = jnp.dot(p.astype(BF16), keys[slot, :, 0:512], preferred_element_type=F32)
        acc[rows, :] = acc[rows, :] * jnp.concatenate([fade] * 4, axis=1) + added

    def attend(zz):
        load_keys(zz, 0)
        fold(0, 0, 2)

    def pair(s, work):
        def one(i, c):
            work(jnp.where(i == 0, (z + 8 - s) % 8, (z + s) % 8))
            return c

        lax.fori_loop(0, jnp.where((s >= 1) & (s <= 3), 2, 1), one, 0)

    def gather_step(s, carry):
        @pl.when(s >= 2)
        def _():
            pair(s - 1, across)

        ring(s, 0)
        ring(s, 1)

        @pl.when(s <= 3)
        def _():
            pair(s - 1, attend)

        return carry

    lax.fori_loop(1, 5, gather_step, 0)

    def att_ring(s, side, u):
        zz = (z + 8 - s) % 8 if side == 0 else (z + s) % 8
        block = att.at[zz, core, u]
        active = (s >= 0) if side == 0 else ((s >= 1) & (s <= 3))

        @pl.when(active & (s > 0))
        def _():
            wait(block, az_recv.at[zz, u])

        @pl.when((s < 3) | ((s == 3) & (core == side)))
        def _():
            to = (z + 1) % 8 if side == 0 else (z + 7) % 8
            send(block, block, az_send.at[0], az_recv.at[zz, u], at(to, xh, core, y, xl))

        @pl.when(active)
        def _():
            send(block, block, as_send.at[0], as_recv.at[zz, u], sibling)

    def finish(u):
        for v in range(4):
            h = u * 4 + v
            rows = slice(h * 128, h * 128 + 128)
            scale = 1.0 / jnp.sum(total[rows, :], axis=1, keepdims=True)
            att[z, core, u, :, v * 128 : v * 128 + 128] = jnp.dot(
                (acc[rows, :] * scale).astype(BF16), uv[h], preferred_element_type=F32
            ).astype(BF16)
        att_ring(0, 0, u)
        att_ring(0, 1, u)

    load_keys((z + 5) % 8, 0)
    load_keys((z + 3) % 8, 1)
    fold(0, 0, 1)
    fold(1, 0, 1)
    across((z + 4) % 8)
    load_keys((z + 4) % 8, 2)
    fold(2, 0, 1)
    finish(0)
    for slot in range(3):
        fold(slot, 1, 1)
    finish(1)
    wait(my_w, w_sem.at[1])

    def multiply(zz):
        for u in range(2):
            wait(att.at[zz, 1 - core, u], as_recv.at[zz, u])

        def product(c, rows):
            return sum(
                lax.dot_general(
                    att[zz, c, u], w[rows, u * 512 : u * 512 + 512], NT, preferred_element_type=F32
                )
                for u in range(2)
            )

        a = product(0, slice(64, 576))
        b = product(1, slice(0, 512))
        part[zz, :, 0:384] = a[:, 0:384].astype(BF16)
        part[zz, :, 384:512] = (a[:, 384:512] + b[:, 0:128]).astype(BF16)
        part[zz, :, 512:896] = b[:, 128:512].astype(BF16)
        for step in range(1, 8):
            y_, xl_ = (y + step // 2) % 4, (xl + step) % 2
            rows = pl.ds(pl.multiple_of((y_ * 2 + xl_) * 16, 16), 16)
            send(
                part.at[zz, rows], got.at[zz, head], c_send.at[0], c_recv.at[zz],
                at(z, xh, core, y_, xl_),
            )
        rows = pl.ds(pl.multiple_of(head * 16, 16), 16)
        got[zz, head] = part[zz, rows, :]

    def reduce(zz):
        wait(got.at[zz, 0:7], c_recv.at[zz])
        whole = got[zz, 0].astype(F32)
        for h in range(1, 8):
            whole = whole + got[zz, h].astype(F32)

        @pl.when(zz == z)
        def _():
            turned[z] = whole.astype(BF16)

        @pl.when(zz != z)
        def _():
            summed[zz] = whole.astype(BF16)
            send(
                summed.at[zz], turned.at[z], t_send.at[0], t_recv.at[z],
                at(zz, xh, core, y, xl),
            )

    def deliver(zz):
        @pl.when(zz != z)
        def _():
            wait(turned.at[zz], t_recv.at[zz])

        for c in range(2):
            window = slice(384 * c, 384 * c + 512)
            own = (zz == head) & (core == c)

            @pl.when(own)
            def _():
                final[head * 2 + core] = turned[zz, :, window]

            @pl.when(jnp.logical_not(own))
            def _():
                send(
                    turned.at[zz, :, window], final.at[head * 2 + core],
                    f_send.at[0], f_recv.at[0], at(z, xh, c, zz // 2, zz % 2),
                )

    def output_step(s, carry):
        @pl.when((s >= 1) & (s <= 4))
        def _():
            for u in range(2):
                att_ring(s, 0, u)
                att_ring(s, 1, u)

        @pl.when(s <= 4)
        def _():
            pair(s, multiply)

        @pl.when((s >= 2) & (s <= 5))
        def _():
            pair(s - 2, reduce)

        @pl.when(s == 5)
        def _():
            reduce((z + 4) % 8)

        @pl.when(s >= 3)
        def _():
            pair(s - 3, deliver)

        return carry

    lax.fori_loop(0, 8, output_step, 0)

    wait(final.at[0:15], f_recv.at[0])
    for c in range(2):

        @pl.when(core == c)
        def _():
            def place(h, carry):
                rows = pl.ds(pl.multiple_of(h * 16, 16), 16)
                v0, v1 = final[h * 2].astype(F32), final[h * 2 + 1].astype(F32)
                empty = jnp.zeros((16, 512), F32)
                v0 = jnp.concatenate([v0, empty], axis=1)
                v1 = jnp.concatenate([v1, empty], axis=1)
                back = 64 * c
                column = lax.broadcasted_iota(jnp.int32, (16, 1024), 1)

                def turn(v, by):
                    return v if by % 1024 == 0 else pltpu.roll(v, by % 1024, 1)

                full = jnp.where(
                    column < 448,
                    jnp.where(column < 224, turn(v0, -back), turn(v1, 224 - back)),
                    jnp.where(column < 672, turn(v0, 224 - back), turn(v1, 448 - back)),
                )
                out_ref[rows, :] = full[:, 0:896].astype(BF16)
                return carry

            lax.fori_loop(0, 8, place, 0)

    wait(mine, x_sem.at[0])
    wait(my_w, w_sem.at[0])
    wait(lat.at[0:7, 0, 0], lz_send.at[0])
    wait(lat.at[0:7, 0, 0], ly_send.at[0])
    wait(lat.at[0:8, 0], ls_send.at[0])
    wait(att.at[0:7, 0], az_send.at[0])
    wait(att.at[0:8, 0], as_send.at[0])
    wait(part.at[0:7], c_send.at[0])
    wait(summed.at[0:7], t_send.at[0])
    wait(final.at[0:15], f_send.at[0])


def shards(queries, latent, key_rope, up_keys, up_values, out_weight, block_order):
    q = jnp.transpose(queries, (1, 2, 0))
    rope = jnp.transpose(key_rope)
    uk = up_keys.reshape(4096, 128)
    uv = up_values.reshape(4096, 128)
    w = jnp.transpose(out_weight)
    vmem = pl.BlockSpec(memory_space=pltpu.VMEM)
    hbm = pl.BlockSpec(memory_space=pl.ANY)
    dma = pltpu.SemaphoreType.DMA
    return pl.pallas_call(
        kernel,
        out_shape=jax.ShapeDtypeStruct((128, 896), BF16),
        in_specs=[hbm] * 7,
        out_specs=vmem,
        scratch_shapes=[
            pltpu.SMEM((64,), jnp.int32),
            pltpu.VMEM((64, 128), BF16),
            pltpu.VMEM((8, 2, 2, 144, 512), BF16),
            pltpu.VMEM((3, 512, 640), BF16),
            pltpu.VMEM((1024, 640), BF16),
            pltpu.VMEM((3, 128, 512), F32),
            pltpu.VMEM((1024, 512), F32),
            pltpu.VMEM((1024, 128), F32),
            pltpu.VMEM((1024, 128), F32),
            pltpu.VMEM((8, 192, 128), BF16),
            pltpu.VMEM((4096, 128), BF16),
            pltpu.VMEM((4096, 128), BF16),
            pltpu.VMEM((8, 512, 128), BF16),
            pltpu.VMEM((8, 512, 128), BF16),
            pltpu.VMEM((576, 1024), BF16),
            pltpu.VMEM((8, 2, 2, 128, 512), BF16),
            pltpu.VMEM((8, 128, 896), BF16),
            pltpu.VMEM((8, 8, 16, 896), BF16),
            pltpu.VMEM((8, 16, 896), BF16),
            pltpu.VMEM((8, 16, 896), BF16),
            pltpu.VMEM((16, 16, 512), BF16),
            dma((7,)), dma((2,)), dma((2,)),
            dma((1,)), dma((8,)), dma((1,)), dma((8,)), dma((1,)), dma((8, 2)),
            dma((1,)), dma((8, 2)), dma((1,)), dma((8, 2)),
            dma((1,)), dma((8,)),
            dma((1,)), dma((8,)),
            dma((1,)), dma((1,)),
        ],
        compiler_params=pltpu.CompilerParams(
            collective_id=0, has_side_effects=True, vmem_limit_bytes=56 * 2**20
        ),
        cost_estimate=pl.CostEstimate(
            flops=25 * 10**9, bytes_accessed=4 * 2**20, transcendentals=4 * 2**20
        ),
        name="latent_attention",
    )(q, latent, rope, uk, uv, w, block_order)


def solution(mesh):
    placed = (
        P("ctx", "head", None),
        P("ctx", None),
        P("ctx", None),
        P(None, "head", None),
        P(None, "head", None),
        P("head", "ctx"),
        P(),
    )
    return jax.shard_map(
        shards, mesh=mesh, in_specs=placed, out_specs=P("ctx", "head"), check_vma=False
    )
```

```python
import functools

import jax
import jax.numpy as jnp
from jax import lax
from jax.experimental import pallas as pl
from jax.experimental.pallas import tpu as pltpu
from jax.sharding import PartitionSpec as P

MESH = pl.DeviceIdType.MESH
F32 = jnp.float32
BF16 = jnp.bfloat16
NT = (((1,), (1,)), ((), ()))
LOW = -1e30


def wait(ref, sem):
    pltpu.make_async_copy(ref, ref, sem).wait()


def kernel(
    q_hbm, lat_hbm, rope_hbm, uk_hbm, uv_hbm, w_hbm, order_hbm, out_ref,
    order_ref, rope_ref, lat, keys, qp, bias, acc, top, total, q_in, uk_in, uv_in, uk, uv, w, att, part, got, summed,
    turned, final,
    in_sem, x_sem, w_sem, lz_send, lz_recv, ly_send, ly_recv, ls_send, ls_recv,
    az_send, az_recv, as_send, as_recv, c_send, c_recv, t_send, t_recv, f_send, f_recv,
):
    ctx, head = lax.axis_index("ctx"), lax.axis_index("head")
    z, xh, core = ctx // 4, (ctx // 2) % 2, ctx % 2
    y, xl = head // 2, head % 2
    factor = (192.0 ** -0.5) * 1.4426950408889634

    def at(z_, xh_, core_, y_, xl_):
        return (z_ * 4 + xh_ * 2 + core_, y_ * 2 + xl_)

    sibling = at(z, xh, 1 - core, y, xl)
    x_next = at(z, 1 - xh, core, y, 1 - xl)
    x_far = at(z, 1 - xh, core, y, xl)

    def send(src, dst, send_sem, recv_sem, device):
        pltpu.make_async_remote_copy(
            src_ref=src, dst_ref=dst, send_sem=send_sem, recv_sem=recv_sem,
            device_id=device, device_id_type=MESH,
        ).start()

    def other_head(step, core_):
        return at(z, xh, core_, (y + step // 2) % 4, (xl + step) % 2)

    barrier = pltpu.get_barrier_semaphore()
    partners = [sibling, x_next, x_far]
    partners += [at((z + step) % 8, xh, core, y, xl) for step in range(1, 8)]
    partners += [other_head(step, c) for step in range(1, 8) for c in (core, 1 - core)]
    for device in partners:
        pl.semaphore_signal(barrier, inc=1, device_id=device, device_id_type=MESH)

    my_w = w.at[pl.ds(pl.multiple_of(64 + 224 * xh, 16), 224)]
    loads = [
        pltpu.make_async_copy(src, dst, in_sem.at[i])
        for i, (src, dst) in enumerate(
            [(q_hbm, q_in), (uk_hbm, uk_in), (uv_hbm, uv_in), (w_hbm, my_w)]
            + [(lat_hbm, lat.at[z, core, xh, 0:128]), (rope_hbm, rope_ref), (order_hbm, order_ref)]
        )
    ]
    for load in loads[4:] + loads[0:4]:
        load.start()

    for load in loads[4:]:
        load.wait()
    rope = jnp.concatenate([rope_ref[...].astype(F32), jnp.zeros((64, 128), F32)], axis=0).T
    rope = rope[0:64, :] + pltpu.roll(rope[64:128, :], 64, 1)
    for g in range(4):
        lat[z, core, xh, 128:144, g * 128 : (g + 1) * 128] = rope[g * 16 : (g + 1) * 16, :].astype(BF16)

    pl.semaphore_wait(barrier, len(partners))
    mine = lat.at[z, core, xh]
    send(mine, mine, x_sem.at[0], x_sem.at[1], x_next)

    carried = (xh + y) % 2

    def ring(s, side):
        zz = (z + 8 - s) % 8 if side == 0 else (z + s) % 8
        block = lat.at[zz, core, carried]
        active = (s <= 4) if side == 0 else ((s >= 1) & (s <= 3))

        @pl.when(active & (s > 0))
        def _():
            wait(block, lz_recv.at[zz])

        @pl.when((s < 3) | ((s == 3) & (core == side)))
        def _():
            to = (z + 1) % 8 if side == 0 else (z + 7) % 8
            send(block, block, lz_send.at[0], lz_recv.at[zz], at(to, xh, core, y, xl))

        down = (s <= 3) | (core == 0) if side == 0 else (s < 0)

        @pl.when(active & (s > 0) & down)
        def _():
            send(block, block, ly_send.at[0], ly_recv.at[zz], at(z, xh, core, (y + 3) % 4, xl))

        @pl.when(active & (s > 0) & jnp.logical_not(down))
        def _():
            send(block, block, ly_send.at[0], ly_recv.at[zz], at(z, xh, core, (y + 1) % 4, xl))

        @pl.when(active)
        def _():
            send(block, block, ls_send.at[0], ls_recv.at[zz, carried], sibling)

    def across(zz):
        block = lat.at[zz, core, 1 - carried]

        @pl.when(zz != z)
        def _():
            wait(block, ly_recv.at[zz])

        send(block, block, ls_send.at[0], ls_recv.at[zz, 1 - carried], sibling)

    @pl.when(carried == xh)
    def _():
        ring(0, 0)
        ring(0, 1)

    wait(mine, x_sem.at[1])

    @pl.when(carried != xh)
    def _():
        ring(0, 0)
        ring(0, 1)

    across(z)
    loads[3].wait()
    send(my_w, my_w, w_sem.at[0], w_sem.at[1], x_far)

    w[0:64, :] = jnp.zeros((64, 1024), BF16)
    w[512:576, :] = jnp.zeros((64, 1024), BF16)

    for load in loads[0:3]:
        load.wait()
    to_row = lax.broadcasted_iota(jnp.int32, (256, 256), 0)
    from_row = lax.broadcasted_iota(jnp.int32, (256, 256), 1)
    turn_rows = jnp.where(
        from_row == (to_row & 31) * 8 + (to_row >> 5), 1.0, 0.0
    ).astype(BF16)

    def by_head(i, carry):
        rows = pl.ds(pl.multiple_of(i * 256, 256), 256)
        both = jnp.concatenate([uk_in[rows, :], uv_in[rows, :]], axis=1)
        both = jnp.dot(turn_rows, both, preferred_element_type=F32).astype(BF16)
        held = pl.ds(pl.multiple_of(i * 32, 32), 32)
        for h in range(8):
            uk[h, held, :] = both[h * 32 : h * 32 + 32, 0:128]
            uv[h, held, :] = both[h * 32 : h * 32 + 32, 128:256]
        return carry

    lax.fori_loop(0, 16, by_head, 0)

    def project(h, carry):
        rows = pl.ds(pl.multiple_of(h * 128, 128), 128)
        q = q_in[h].astype(F32)
        plain = q[0:128, :].T.astype(BF16)
        qp[rows, 0:512] = lax.dot_general(
            plain, uk[h], NT, preferred_element_type=F32
        ).astype(BF16)
        turned_rope = jnp.concatenate([q[128:192, :], jnp.zeros((64, 128), F32)], axis=0).T
        qp[rows, 512:640] = turned_rope.astype(BF16)
        return carry

    lax.fori_loop(0, 8, project, 0)
    top[...] = jnp.full_like(top, LOW)
    total[...] = jnp.zeros_like(total)
    acc[...] = jnp.zeros_like(acc)

    lane = lax.broadcasted_iota(jnp.int32, (8, 512), 1)
    row = lax.broadcasted_iota(jnp.int32, (128, 512), 0)

    def load_keys(zz, slot):
        for x in range(2):
            wait(lat.at[zz, 1 - core, x], ls_recv.at[zz, x])
        place = jnp.zeros((8, 512), jnp.int32)
        for c in range(2):
            for x in range(2):
                n = c * 2 + x
                for half in range(2):
                    block = order_ref[zz * 8 + x * 4 + c * 2 + half] * 64
                    place = jnp.where((lane >> 6) == n * 2 + half, block + (lane & 63), place)
                keys[slot, n * 128 : (n + 1) * 128, 0:512] = lat[zz, c, x, 0:128, :]
                for g in range(4):
                    pair = lat[zz, c, x, 128:144, g * 128 : (g + 1) * 128]
                    keys[slot, n * 128 + g * 16 : n * 128 + g * 16 + 16, 512:640] = pair
                    turn = pltpu.roll(pair.astype(F32), 64, 1).astype(BF16)
                    keys[slot, n * 128 + 64 + g * 16 : n * 128 + 64 + g * 16 + 16, 512:640] = turn
        own = row + jnp.where(
            row < 64, order_ref[ctx * 2] * 64, order_ref[ctx * 2 + 1] * 64 - 64
        )
        bias[slot] = jnp.where(place[0:1, :] <= own, 0.0, LOW)

    def fold(slot, first, count):
        rows = slice(first * 512, (first + count) * 512)
        s = lax.dot_general(qp[rows, :], keys[slot], NT, preferred_element_type=F32)
        s = s + jnp.concatenate([bias[slot]] * (4 * count), axis=0)
        old = top[rows, :]
        new = jnp.maximum(old, jnp.max(s, axis=1, keepdims=True))
        top[rows, :] = new
        p = jnp.exp2((s - jnp.concatenate([new] * 4, axis=1)) * factor)
        fade = jnp.exp2((old - new) * factor)
        total[rows, :] = total[rows, :] * fade + (
            (p[:, 0:128] + p[:, 128:256]) + (p[:, 256:384] + p[:, 384:512])
        )
        added = jnp.dot(p.astype(BF16), keys[slot, :, 0:512], preferred_element_type=F32)
        acc[rows, :] = acc[rows, :] * jnp.concatenate([fade] * 4, axis=1) + added

    def attend(zz):
        load_keys(zz, 0)
        fold(0, 0, 2)

    def pair(s, work):
        def one(i, c):
            work(jnp.where(i == 0, (z + 8 - s) % 8, (z + s) % 8))
            return c

        lax.fori_loop(0, jnp.where((s >= 1) & (s <= 3), 2, 1), one, 0)

    def gather_step(s, carry):
        @pl.when(s >= 2)
        def _():
            pair(s - 1, across)

        ring(s, 0)
        ring(s, 1)

        @pl.when(s <= 3)
        def _():
            pair(s - 1, attend)

        return carry

    lax.fori_loop(1, 5, gather_step, 0)

    def att_ring(s, side, u):
        zz = (z + 8 - s) % 8 if side == 0 else (z + s) % 8
        block = att.at[zz, core, u]
        active = (s >= 0) if side == 0 else ((s >= 1) & (s <= 3))

        @pl.when(active & (s > 0))
        def _():
            wait(block, az_recv.at[zz, u])

        @pl.when((s < 3) | ((s == 3) & (core == side)))
        def _():
            to = (z + 1) % 8 if side == 0 else (z + 7) % 8
            send(block, block, az_send.at[0], az_recv.at[zz, u], at(to, xh, core, y, xl))

        @pl.when(active)
        def _():
            send(block, block, as_send.at[0], as_recv.at[zz, u], sibling)

    def finish(u):
        for v in range(4):
            h = u * 4 + v
            rows = slice(h * 128, h * 128 + 128)
            scale = 1.0 / jnp.sum(total[rows, :], axis=1, keepdims=True)
            att[z, core, u, :, v * 128 : v * 128 + 128] = jnp.dot(
                (acc[rows, :] * scale).astype(BF16), uv[h], preferred_element_type=F32
            ).astype(BF16)
        att_ring(0, 0, u)
        att_ring(0, 1, u)

    load_keys((z + 5) % 8, 0)
    load_keys((z + 3) % 8, 1)
    fold(0, 0, 1)
    fold(1, 0, 1)
    across((z + 4) % 8)
    load_keys((z + 4) % 8, 2)
    fold(2, 0, 1)
    finish(0)
    for slot in range(3):
        fold(slot, 1, 1)
    finish(1)
    wait(my_w, w_sem.at[1])

    def multiply(zz):
        for u in range(2):
            wait(att.at[zz, 1 - core, u], as_recv.at[zz, u])

        def product(c, rows):
            return sum(
                lax.dot_general(
                    att[zz, c, u], w[rows, u * 512 : u * 512 + 512], NT, preferred_element_type=F32
                )
                for u in range(2)
            )

        a = product(0, slice(64, 576))
        b = product(1, slice(0, 512))
        part[zz, :, 0:384] = a[:, 0:384].astype(BF16)
        part[zz, :, 384:512] = (a[:, 384:512] + b[:, 0:128]).astype(BF16)
        part[zz, :, 512:896] = b[:, 128:512].astype(BF16)
        for step in (5, 4, 3, 7, 2, 6, 1):
            y_, xl_ = (y + step // 2) % 4, (xl + step) % 2
            rows = pl.ds(pl.multiple_of((y_ * 2 + xl_) * 16, 16), 16)
            send(
                part.at[zz, rows], got.at[zz, head], c_send.at[0], c_recv.at[zz],
                at(z, xh, core, y_, xl_),
            )
        rows = pl.ds(pl.multiple_of(head * 16, 16), 16)
        got[zz, head] = part[zz, rows, :]

    def reduce(zz):
        wait(got.at[zz, 0:7], c_recv.at[zz])
        whole = got[zz, 0].astype(F32)
        for h in range(1, 8):
            whole = whole + got[zz, h].astype(F32)

        @pl.when(zz == z)
        def _():
            turned[z] = whole.astype(BF16)

        @pl.when(zz != z)
        def _():
            summed[zz] = whole.astype(BF16)
            send(
                summed.at[zz], turned.at[z], t_send.at[0], t_recv.at[z],
                at(zz, xh, core, y, xl),
            )

    def deliver(zz):
        @pl.when(zz != z)
        def _():
            wait(turned.at[zz], t_recv.at[zz])

        for c in range(2):
            window = slice(384 * c, 384 * c + 512)
            own = (zz == head) & (core == c)

            @pl.when(own)
            def _():
                final[head * 2 + core] = turned[zz, :, window]

            @pl.when(jnp.logical_not(own))
            def _():
                send(
                    turned.at[zz, :, window], final.at[head * 2 + core],
                    f_send.at[0], f_recv.at[0], at(z, xh, c, zz // 2, zz % 2),
                )

    def output_step(s, carry):
        @pl.when((s >= 1) & (s <= 4))
        def _():
            for u in range(2):
                att_ring(s, 0, u)
                att_ring(s, 1, u)

        @pl.when(s <= 4)
        def _():
            pair(s, multiply)

        @pl.when((s >= 2) & (s <= 5))
        def _():
            pair(s - 2, reduce)

        @pl.when(s == 5)
        def _():
            reduce((z + 4) % 8)

        @pl.when(s >= 3)
        def _():
            pair(s - 3, deliver)

        return carry

    lax.fori_loop(0, 8, output_step, 0)

    wait(final.at[0:15], f_recv.at[0])
    for c in range(2):

        @pl.when(core == c)
        def _():
            def place(h, carry):
                rows = pl.ds(pl.multiple_of(h * 16, 16), 16)
                v0, v1 = final[h * 2].astype(F32), final[h * 2 + 1].astype(F32)
                empty = jnp.zeros((16, 512), F32)
                v0 = jnp.concatenate([v0, empty], axis=1)
                v1 = jnp.concatenate([v1, empty], axis=1)
                back = 64 * c
                column = lax.broadcasted_iota(jnp.int32, (16, 1024), 1)

                def turn(v, by):
                    return v if by % 1024 == 0 else pltpu.roll(v, by % 1024, 1)

                full = jnp.where(
                    column < 448,
                    jnp.where(column < 224, turn(v0, -back), turn(v1, 224 - back)),
                    jnp.where(column < 672, turn(v0, 224 - back), turn(v1, 448 - back)),
                )
                out_ref[rows, :] = full[:, 0:896].astype(BF16)
                return carry

            lax.fori_loop(0, 8, place, 0)

    wait(mine, x_sem.at[0])
    wait(my_w, w_sem.at[0])
    wait(lat.at[0:7, 0, 0], lz_send.at[0])
    wait(lat.at[0:7, 0, 0], ly_send.at[0])
    wait(lat.at[0:8, 0], ls_send.at[0])
    wait(att.at[0:7, 0], az_send.at[0])
    wait(att.at[0:8, 0], as_send.at[0])
    wait(part.at[0:7], c_send.at[0])
    wait(summed.at[0:7], t_send.at[0])
    wait(final.at[0:15], f_send.at[0])


def shards(queries, latent, key_rope, up_keys, up_values, out_weight, block_order):
    q = jnp.transpose(queries, (1, 2, 0))
    rope = jnp.transpose(key_rope)
    uk = up_keys.reshape(4096, 128)
    uv = up_values.reshape(4096, 128)
    w = jnp.transpose(out_weight)
    vmem = pl.BlockSpec(memory_space=pltpu.VMEM)
    hbm = pl.BlockSpec(memory_space=pl.ANY)
    dma = pltpu.SemaphoreType.DMA
    return pl.pallas_call(
        kernel,
        out_shape=jax.ShapeDtypeStruct((128, 896), BF16),
        in_specs=[hbm] * 7,
        out_specs=vmem,
        scratch_shapes=[
            pltpu.SMEM((64,), jnp.int32),
            pltpu.VMEM((64, 128), BF16),
            pltpu.VMEM((8, 2, 2, 144, 512), BF16),
            pltpu.VMEM((3, 512, 640), BF16),
            pltpu.VMEM((1024, 640), BF16),
            pltpu.VMEM((3, 128, 512), F32),
            pltpu.VMEM((1024, 512), F32),
            pltpu.VMEM((1024, 128), F32),
            pltpu.VMEM((1024, 128), F32),
            pltpu.VMEM((8, 192, 128), BF16),
            pltpu.VMEM((4096, 128), BF16),
            pltpu.VMEM((4096, 128), BF16),
            pltpu.VMEM((8, 512, 128), BF16),
            pltpu.VMEM((8, 512, 128), BF16),
            pltpu.VMEM((576, 1024), BF16),
            pltpu.VMEM((8, 2, 2, 128, 512), BF16),
            pltpu.VMEM((8, 128, 896), BF16),
            pltpu.VMEM((8, 8, 16, 896), BF16),
            pltpu.VMEM((8, 16, 896), BF16),
            pltpu.VMEM((8, 16, 896), BF16),
            pltpu.VMEM((16, 16, 512), BF16),
            dma((7,)), dma((2,)), dma((2,)),
            dma((1,)), dma((8,)), dma((1,)), dma((8,)), dma((1,)), dma((8, 2)),
            dma((1,)), dma((8, 2)), dma((1,)), dma((8, 2)),
            dma((1,)), dma((8,)),
            dma((1,)), dma((8,)),
            dma((1,)), dma((1,)),
        ],
        compiler_params=pltpu.CompilerParams(
            collective_id=0, has_side_effects=True, vmem_limit_bytes=56 * 2**20
        ),
        cost_estimate=pl.CostEstimate(
            flops=25 * 10**9, bytes_accessed=4 * 2**20, transcendentals=4 * 2**20
        ),
        name="latent_attention",
    )(q, latent, rope, uk, uv, w, block_order)


def solution(mesh):
    placed = (
        P("ctx", "head", None),
        P("ctx", None),
        P("ctx", None),
        P(None, "head", None),
        P(None, "head", None),
        P("head", "ctx"),
        P(),
    )
    return jax.shard_map(
        shards, mesh=mesh, in_specs=placed, out_specs=P("ctx", "head"), check_vma=False
    )
```
